128 devices in a mesh: region: 64 (over z, y_lo, x, core), level: 2 (over y_hi).
Axes of the slice: x: 4, y: 4 (y_hi: 2, y_lo: 2; y = y_hi * 2 + y_lo), z: 4, core: 2. Of those that a mesh axis runs over, the one named last changes fastest.
Arguments:
- prior_samples: bfloat16 [256, 16, 98304], P('region', 'level'), may hold values from -6 to 6
- measured_site: int32 [32768], P('region'), may hold values from 0 to 24575
- measured_datum: float32 [32768], P('region'), may hold values from -6 to 6
- inverse_variance: float32 [32768], P('region'), may hold values from 0.5 to 8
- active_slots: int32 [64], P('region'), may hold values from 256 to 512
- cutoff_distance: int32 [64], P('region'), may hold values from 128 to 256
Outputs:
- analysis: bfloat16 [256, 16, 98304], P('region', 'level')
The draws below stay inside these ranges and needn't reach their ends.
Inputs may be any that keep to these rules, and one draw needn't show every extreme that they name: measured_site[o] = level * 1536 + cell within its region, for a level below 16. Slots of region r at or past active_slots[r] are empty and are ignored.
All inputs are finite; a program needn't handle non-finite values.
Results may differ from the reference program's by a relative error of at most 0.00115.
The reference program's roundings to bfloat16 on the way count: a program that leaves them out, or rounds other values in their place, can miss the bound.
Values may be sent and summed in bfloat16 or wider, within the bound.
A program may use at most 256 MiB of HBM per device.

```python
import math
import jax
import jax.numpy as jnp
from jax import lax

SAMPLE_SIZE = 256
COARSE = 6
SPACING = 256
OBS_DEV = 512
NS_ITERS = 5
PTS_DEV = 1536
REGIONS = 64
HEIGHT_TIERS = 16
GRID_SITES = 98304
NOBS = 32768


def plant(values, own_key, smallest, high):
    longest = values.shape.index(max(values.shape))
    spots = []
    for shift in (0, 1):
        where = [jax.random.randint(jax.random.fold_in(own_key, axis), (), 0, length) for axis, length in enumerate(values.shape)]
        where[longest] = (where[longest] + shift) % values.shape[longest]
        spots.append(tuple(where))
    return values.at[spots[0]].set(smallest).at[spots[1]].set(high)


def levels(rng, extent, split, least, top_value):
    level, own = 1.0, jax.random.fold_in(rng, 6)
    for dim, parts in split:
        steps = jnp.exp(jax.random.uniform(jax.random.fold_in(own, dim), (parts,), jnp.float32, least / len(split), top_value / len(split)))
        level = level * jnp.repeat(steps, extent[dim] // parts).reshape([-1 if axis == dim else 1 for axis in range(len(extent))])
    return level


def noise(own_key, shape, scale, bound, cuts=(), kind=jnp.bfloat16):
    drawn = scale * jax.random.normal(own_key, shape, jnp.float32)
    if cuts:
        drawn = drawn * levels(own_key, shape, cuts, -0.22, 0.18)
    return jnp.clip(drawn, -bound, bound).astype(kind)


def setup_inputs(seed: int = 0) -> dict:
    streams_of = jax.random.split(jax.random.key(seed), 7)
    prior_samples = noise(streams_of[0], (SAMPLE_SIZE, HEIGHT_TIERS, GRID_SITES), 1.0, 6.0, ((0, 64), (1, 2)))
    measured_site = plant(jax.random.randint(streams_of[1], (NOBS,), 0, HEIGHT_TIERS * PTS_DEV), jax.random.fold_in(streams_of[1], 1), 0, (HEIGHT_TIERS * PTS_DEV) - 1).astype(jnp.int32)
    measured_datum = noise(streams_of[2], (NOBS,), 1.0, 6.0, ((0, 64),), jnp.float32)
    inverse_variance = jnp.clip(jnp.exp(math.log(8.0) - 2.7725887 * jax.random.uniform(streams_of[3], (NOBS,), jnp.float32) ** levels(streams_of[3], (NOBS,), ((0, 64),), -0.2, 0.2)), 0.5, 8.0)
    active_slots = plant(jax.random.randint(streams_of[4], (REGIONS,), OBS_DEV // 2, OBS_DEV + 1), jax.random.fold_in(streams_of[4], 1), OBS_DEV // 2, OBS_DEV).astype(jnp.int32)
    cutoff_distance = plant(jax.random.randint(streams_of[5], (REGIONS,), SPACING // 2, SPACING + 1), jax.random.fold_in(streams_of[5], 1), SPACING // 2, SPACING).astype(jnp.int32)
    return dict(prior_samples=prior_samples, measured_site=measured_site, measured_datum=measured_datum, inverse_variance=inverse_variance, active_slots=active_slots, cutoff_distance=cutoff_distance)


inflation = 1.1

def local_products(window, records, radius_cells):
    values = window.astype(jnp.float32)
    centre = lax.optimization_barrier(jnp.mean(values, axis=0))
    departure = values - centre[None, :]
    innovation = records[3] * (records[0] - centre)
    coarse = (SPACING // 2 + SPACING * jnp.arange(COARSE, dtype=jnp.int32)).astype(jnp.float32)
    distance = (records[2][None, :] - coarse[:, None]) / radius_cells
    root_weight = jnp.sqrt(jnp.exp(-0.5 * distance * distance) * records[1][None, :])
    scaled = (departure[None, :, :] * root_weight[:, None, :]).astype(jnp.bfloat16)
    weighted = (root_weight * innovation[None, :]).astype(jnp.bfloat16)
    scaled_wide = scaled.astype(jnp.float32)
    gram_matrix = jnp.einsum('cjo,cmo->cjm', scaled_wide, scaled_wide, precision=lax.Precision.HIGHEST)
    right_side = jnp.einsum('cjo,co->cj', scaled_wide, weighted.astype(jnp.float32), precision=lax.Precision.HIGHEST)
    return (gram_matrix, right_side)

def ensemble_weights(gram_matrix, right_side):
    sample_runs = gram_matrix.shape[-1]
    identity = jnp.eye(sample_runs, dtype=jnp.float32)
    shifted = gram_matrix + (sample_runs - 1) / inflation * identity[None]
    frobenius = jnp.sqrt(lax.optimization_barrier(jnp.sum(shifted * shifted, axis=(1, 2))))
    iterate = shifted / frobenius[:, None, None]
    inverse = jnp.broadcast_to(identity, shifted.shape)
    for turn_index in range(NS_ITERS):
        factor = 1.5 * identity[None] - 0.5 * jnp.matmul(inverse, iterate, precision=lax.Precision.HIGHEST)
        iterate = jnp.matmul(iterate, factor, precision=lax.Precision.HIGHEST)
        inverse = jnp.matmul(factor, inverse, precision=lax.Precision.HIGHEST)
    spread = inverse * jnp.sqrt((sample_runs - 1.0) / frobenius)[:, None, None]
    inner_step = jnp.einsum('cjm,cm->cj', inverse, right_side, precision=lax.Precision.HIGHEST)
    centre = jnp.einsum('cjm,cm->cj', inverse, inner_step, precision=lax.Precision.HIGHEST) / frobenius[:, None]
    weights = spread + centre[:, :, None]
    return (weights - lax.optimization_barrier(jnp.mean(weights, axis=1, keepdims=True)) + 1.0 / sample_runs).astype(jnp.bfloat16)

def transform(vertical_profiles, extended):
    sample_runs, height_tiers, grid_sites = vertical_profiles.shape
    half_block = grid_sites // (2 * COARSE)
    shaped = vertical_profiles.astype(jnp.float32).reshape(sample_runs, height_tiers, COARSE, 2, half_block)
    ext_wide = extended.astype(jnp.float32)
    middle = jnp.einsum('jlmqp,mjk->klmqp', shaped, ext_wide[1:COARSE + 1], precision=lax.Precision.HIGHEST)
    before = jnp.einsum('jlmp,mjk->klmp', shaped[:, :, :, 0], ext_wide[:COARSE], precision=lax.Precision.HIGHEST)
    beyond = jnp.einsum('jlmp,mjk->klmp', shaped[:, :, :, 1], ext_wide[2:], precision=lax.Precision.HIGHEST)
    offset = jnp.arange(half_block, dtype=jnp.float32)
    frac_low = (offset + half_block) / (2 * half_block)
    frac_high = offset / (2 * half_block)
    low_half = (1.0 - frac_low) * before + frac_low * middle[:, :, :, 0]
    high_half = (1.0 - frac_high) * middle[:, :, :, 1] + frac_high * beyond
    return jnp.stack([low_half, high_half], axis=3).reshape(sample_runs, height_tiers, grid_sites).astype(jnp.bfloat16)

def reference(prior_samples, measured_site, measured_datum, inverse_variance, active_slots, cutoff_distance):
    sample_runs, height_tiers, grand_accumulated = prior_samples.shape
    grid_sites = COARSE * SPACING
    regions = grand_accumulated // grid_sites
    slots = measured_site.shape[0] // regions
    slot_index = jnp.arange(regions * slots, dtype=jnp.int32)
    region_of = (slot_index // slots).astype(jnp.int32)
    live = slot_index % slots < active_slots[region_of]
    level_of = measured_site // grid_sites
    point_of = measured_site % grid_sites
    linear_offset = (level_of * grand_accumulated + region_of * grid_sites + point_of).astype(jnp.int32)
    sample_fields = jnp.take(prior_samples.reshape(sample_runs, height_tiers * grand_accumulated), linear_offset, axis=1)
    sample_fields = jnp.where(live[None, :], sample_fields, jnp.zeros_like(sample_fields))
    live_f = live.astype(jnp.float32)
    records = jnp.stack([measured_datum, inverse_variance * live_f, point_of.astype(jnp.float32), live_f])
    ensemble_by = sample_fields.reshape(sample_runs, regions, slots)
    records_by = records.reshape(4, regions, slots)
    shifts = jnp.array([-grid_sites, 0, grid_sites], dtype=jnp.float32)

    def one_region(patch_ordinal):
        neighbours = jnp.stack([(patch_ordinal - 1) % regions, patch_ordinal, (patch_ordinal + 1) % regions]).astype(jnp.int32)
        window = jnp.take(ensemble_by, neighbours, axis=1).reshape(sample_runs, 3 * slots)
        near = jnp.take(records_by, neighbours, axis=1)
        position = near[2] + shifts[:, None]
        near = jnp.stack([near[0], near[1], position, near[3]]).reshape(4, 3 * slots)
        gram_matrix, right_side = local_products(window, near, cutoff_distance[patch_ordinal].astype(jnp.float32))
        return ensemble_weights(gram_matrix, right_side)
    weights = lax.map(one_region, jnp.arange(regions, dtype=jnp.int32))
    extended = jnp.concatenate([jnp.roll(weights[:, -1:], 1, axis=0), weights, jnp.roll(weights[:, :1], -1, axis=0)], axis=1)

    def one_block(region_item):
        patch_ordinal, ext_block = region_item
        vertical_profiles = lax.dynamic_slice_in_dim(prior_samples, (patch_ordinal * grid_sites).astype(jnp.int32), grid_sites, axis=2)
        return transform(vertical_profiles, ext_block)
    blocks = lax.map(one_block, (jnp.arange(regions, dtype=jnp.int32), extended))
    return jnp.transpose(blocks, (1, 2, 0, 3)).reshape(sample_runs, height_tiers, grand_accumulated)
```

```python
import functools
import itertools

import jax
import jax.numpy as jnp
from jax import lax
from jax.experimental import pallas as pl
from jax.experimental.pallas import tpu as pltpu
from jax.sharding import PartitionSpec as P

COARSE = 6
SPACING = 256
NS_ITERS = 5


inflation = 1.1


def in_blocks(value, dim, peers):
    shape = value.shape
    pieces = value.reshape(*shape[:dim], peers, shape[dim] // peers, *shape[dim + 1 :])
    return jnp.moveaxis(pieces, dim, 0)


def edges_of(length, count):
    lap = length // count
    if lap >= 8:
        lap -= lap % 8
    return [lap * k for k in range(1, count)]


def laid_out(pieces, dim):
    shape = list(pieces.shape[1:])
    shape[dim] *= pieces.shape[0]
    return jnp.moveaxis(pieces, 0, dim).reshape(shape)


def several_exchanges(value, axis, pieces, split_dim, concat_dim):
    blocks = in_blocks(value, split_dim, lax.axis_size(axis))
    split_at = max(range(1, max(2, blocks.ndim - 1)), key=lambda d: blocks.shape[d])
    finished = []
    for piece in jnp.split(blocks, edges_of(blocks.shape[split_at], pieces), axis=split_at):
        if piece.size:
            finished.append(lax.all_to_all(piece, axis, split_axis=0, concat_axis=0, tiled=True))
    return laid_out(jnp.concatenate(finished, axis=split_at), concat_dim)


def copy_for_each(value, axis):
    peers = lax.axis_size(axis)
    return lax.all_to_all(
        jnp.broadcast_to(value[None], (peers, *value.shape)), axis, 0, 0, tiled=True
    )


def over_copies(value, axis):
    return copy_for_each(value, axis).astype(jnp.float32).sum(axis=0)


def with_halo(block, sides, width):
    for axis, dim in sides:
        count = lax.axis_size(axis)
        forward = [(i, i + 1) for i in range(count - 1)]
        forward.append((count - 1, 0))
        backward = [(target, source) for source, target in forward]
        low = lax.ppermute(
            lax.slice_in_dim(block, block.shape[dim] - width, None, axis=dim), axis, forward
        )
        high = lax.ppermute(lax.slice_in_dim(block, 0, width, axis=dim), axis, backward)
        block = jnp.concatenate([low, block, high], axis=dim)
    return block


def local_products(window, records, radius_cells):
    values = window.astype(jnp.float32)
    centre = jnp.mean(values, axis=0)
    departure = values - centre[None, :]
    innovation = records[3] * (records[0] - centre)
    coarse = (SPACING // 2 + SPACING * jnp.arange(COARSE, dtype=jnp.int32)).astype(jnp.float32)
    distance = (records[2][None, :] - coarse[:, None]) / radius_cells
    root_weight = jnp.sqrt(jnp.exp(-0.5 * distance * distance) * records[1][None, :])
    scaled = (departure[None, :, :] * root_weight[:, None, :]).astype(jnp.bfloat16)
    weighted = (root_weight * innovation[None, :]).astype(jnp.bfloat16)
    gram_matrix = jnp.einsum("cjo,cmo->cjm", scaled, scaled, preferred_element_type=jnp.float32)
    right_side = jnp.einsum("cjo,co->cj", scaled, weighted, preferred_element_type=jnp.float32)
    return (gram_matrix, right_side)


def ensemble_weights(gram_matrix, right_side):
    sample_runs = gram_matrix.shape[-1]
    identity = jnp.eye(sample_runs, dtype=jnp.float32)
    shifted = gram_matrix + (sample_runs - 1) / inflation * identity[None]
    frobenius = jnp.sqrt(jnp.sum(shifted * shifted, axis=(1, 2)))
    iterate = shifted / frobenius[:, None, None]
    inverse = jnp.broadcast_to(identity, shifted.shape)
    for turn_index in range(NS_ITERS):
        factor = 1.5 * identity[None] - 0.5 * jnp.matmul(
            inverse, iterate, precision=lax.Precision.HIGHEST
        )
        iterate = jnp.matmul(iterate, factor, precision=lax.Precision.HIGHEST)
        inverse = jnp.matmul(factor, inverse, precision=lax.Precision.HIGHEST)
    spread = inverse * jnp.sqrt((sample_runs - 1.0) / frobenius)[:, None, None]
    inner_step = jnp.einsum("cjm,cm->cj", inverse, right_side, precision=lax.Precision.HIGHEST)
    centre = (
        jnp.einsum("cjm,cm->cj", inverse, inner_step, precision=lax.Precision.HIGHEST)
        / frobenius[:, None]
    )
    weights = spread + centre[:, :, None]
    return (weights - jnp.mean(weights, axis=1, keepdims=True) + 1.0 / sample_runs).astype(
        jnp.bfloat16
    )


MESH = pl.DeviceIdType.MESH
RING = 4
GROUP = 64
OWN = 4
LEVELS = 8
CELLS = COARSE * SPACING
HALF = SPACING // 2
HALVES = CELLS // HALF
PIECES = 3


def link_load(offset):
    dz, dy, dx, _ = offset
    return [float(dx in (1, 2)), float(dx in (3, 2)), float(dz in (1, 2)), float(dz in (3, 2)), float(dy)]


def balanced_order():
    left = [o for o in itertools.product(range(4), range(2), range(4), range(2)) if any(o)]
    total, order = [0.0] * 5, []
    while left:
        best = None
        for offset in left:
            after = [0.8 * a + b for a, b in zip(total, link_load(offset))]
            middle = sum(after) / 5
            score = sum((v - middle) ** 2 for v in after) - 0.3 * sum(link_load(offset))
            if best is None or score < best[0] - 1e-9:
                best = (score, offset, after)
        order.append(best[1])
        left.remove(best[1])
        total = best[2]
    return order


def peer_at(me, offset):
    core, x, y, z = me % 2, me // 2 % 4, me // 8 % 2, me // 16
    sign = 1 - 2 * core
    dz, dy, dx, dc = offset
    z, y = (z + sign * dz + 4) % 4, (y + dy) % 2
    x, core = (x + sign * dx + 4) % 4, (core + dc) % 2
    return ((z * 2 + y) * 4 + x) * 2 + core


def greet(me, level):
    barrier = pltpu.get_barrier_semaphore()

    @pl.loop(1, GROUP)
    def _(step):
        pl.semaphore_signal(barrier, inc=1, device_id=(lax.rem(me + step, GROUP), level), device_id_type=MESH)

    pl.semaphore_wait(barrier, GROUP - 1)


def gather_kernel(own, patch, send_sem, recv_sem, local_sem):
    me, level = lax.axis_index("region"), lax.axis_index("level")
    greet(me, level)
    mine = pltpu.make_async_copy(
        own.at[:, :, pl.ds(pl.multiple_of(me * CELLS, CELLS), CELLS)], patch.at[pl.ds(OWN * me, OWN)], local_sem
    )
    mine.start()
    width = CELLS // PIECES

    @pl.loop(0, PIECES)
    def _(piece):
        at = pl.multiple_of(piece * width, width)
        for offset in balanced_order():
            peer = peer_at(me, offset)
            pltpu.make_async_remote_copy(
                src_ref=own.at[:, :, pl.ds(pl.multiple_of(peer * CELLS + at, width), width)],
                dst_ref=patch.at[pl.ds(OWN * me, OWN), :, pl.ds(at, width)],
                send_sem=send_sem,
                recv_sem=recv_sem,
                device_id=(peer, level),
                device_id_type=MESH,
            ).start()

    mine.wait()
    others = patch.at[pl.ds(0, OWN * (GROUP - 1))]
    pltpu.make_async_copy(others, others, recv_sem).wait()
    pltpu.make_async_copy(others, others, send_sem).wait()


def gather_members(own):
    return pl.pallas_call(
        gather_kernel,
        out_shape=jax.ShapeDtypeStruct((OWN * GROUP, LEVELS, CELLS), jnp.bfloat16),
        in_specs=[pl.BlockSpec(memory_space=pl.ANY)],
        out_specs=pl.BlockSpec(memory_space=pl.ANY),
        scratch_shapes=[pltpu.SemaphoreType.DMA] * 3,
        compiler_params=pltpu.CompilerParams(collective_id=0, has_side_effects=True),
    )(own)


def analyse_half(half, patch, mixing, result, wide_in, wide_out):
    members = OWN * GROUP
    at = pl.multiple_of(half * HALF, HALF)
    wide_in[...] = patch[:, :, pl.ds(at, HALF)].astype(jnp.float32).reshape(members * LEVELS, HALF)
    first = (half + 1) // 2
    low, high = mixing[first], mixing[first + 1]
    lane = lax.broadcasted_iota(jnp.int32, (1, HALF), 1)
    frac = (lane + jnp.where(half % 2 == 0, HALF, 0)).astype(jnp.float32) / SPACING
    frac = jnp.concatenate([frac, frac], axis=1)
    for tier in range(0, LEVELS, 2):
        field = jnp.concatenate(
            [wide_in[pl.ds(tier + t, members, stride=LEVELS), :] for t in range(2)], axis=1
        ).astype(jnp.bfloat16)
        before = jnp.dot(low, field, preferred_element_type=jnp.float32)
        beyond = jnp.dot(high, field, preferred_element_type=jnp.float32)
        mixed = (1.0 - frac) * before + frac * beyond
        for t in range(2):
            wide_out[pl.ds(tier + t, members, stride=LEVELS), :] = mixed[:, t * HALF : (t + 1) * HALF]
    result[:, :, pl.ds(at, HALF)] = wide_out[...].reshape(members, LEVELS, HALF).astype(jnp.bfloat16)


def analyse_kernel(patch, mixing, out, result, wide_in, wide_out, send_sem, recv_sem, local_sem):
    me, level = lax.axis_index("region"), lax.axis_index("level")
    greet(me, level)
    per_piece = HALVES // PIECES
    width = CELLS // PIECES

    @pl.loop(0, PIECES)
    def _(piece):
        @pl.loop(0, per_piece)
        def _(step):
            analyse_half(piece * per_piece + step, patch, mixing, result, wide_in, wide_out)

        at = pl.multiple_of(piece * width, width)
        for offset in balanced_order():
            peer = peer_at(me, offset)
            pltpu.make_async_remote_copy(
                src_ref=result.at[pl.ds(OWN * peer, OWN), :, pl.ds(at, width)],
                dst_ref=out.at[:, :, pl.ds(pl.multiple_of(me * CELLS + at, width), width)],
                send_sem=send_sem,
                recv_sem=recv_sem,
                device_id=(peer, level),
                device_id_type=MESH,
            ).start()

    mine = pltpu.make_async_copy(
        result.at[pl.ds(OWN * me, OWN)], out.at[:, :, pl.ds(pl.multiple_of(me * CELLS, CELLS), CELLS)], local_sem
    )
    mine.start()
    mine.wait()
    others = result.at[pl.ds(0, OWN * (GROUP - 1))]
    pltpu.make_async_copy(others, others, recv_sem).wait()
    pltpu.make_async_copy(others, others, send_sem).wait()


def analyse(patch, mixing):
    members = OWN * GROUP
    return pl.pallas_call(
        analyse_kernel,
        out_shape=jax.ShapeDtypeStruct((OWN, LEVELS, GROUP * CELLS), jnp.bfloat16),
        in_specs=[pl.BlockSpec(memory_space=pltpu.VMEM)] * 2,
        out_specs=pl.BlockSpec(memory_space=pl.ANY),
        scratch_shapes=[
            pltpu.VMEM((members, LEVELS, CELLS), jnp.bfloat16),
            pltpu.VMEM((members * LEVELS, HALF), jnp.float32),
            pltpu.VMEM((members * LEVELS, HALF), jnp.float32),
        ]
        + [pltpu.SemaphoreType.DMA] * 3,
        compiler_params=pltpu.CompilerParams(
            collective_id=1, has_side_effects=True, vmem_limit_bytes=40 * 2**20
        ),
    )(patch, mixing)


def local(
    prior_samples, measured_site, measured_datum, inverse_variance, active_slots, cutoff_distance
):
    sample_slice, height_tiers, grand_accumulated = prior_samples.shape
    grid_sites = COARSE * SPACING
    slots = measured_site.shape[0]
    level_index = lax.axis_index("level")
    level_first = level_index * height_tiers
    live = jnp.arange(slots, dtype=jnp.int32) < active_slots[0]
    level_of = measured_site // grid_sites
    point_of = measured_site % grid_sites
    owned = live & (level_of // height_tiers == level_index)
    patch_tile = gather_members(prior_samples)
    sample_runs = patch_tile.shape[0]
    linear_offset = jnp.clip(
        (level_of - level_first) * grid_sites + point_of, 0, height_tiers * grid_sites - 1
    )
    observed = jnp.take(
        patch_tile.reshape(sample_runs, height_tiers * grid_sites), linear_offset, axis=1
    )
    observed = jnp.where(owned[None, :], observed, jnp.zeros_like(observed))
    observed = (
        over_copies(observed.astype(jnp.float32).astype(jnp.bfloat16), "level")
        .astype(jnp.float32)
        .astype(jnp.bfloat16)
    )
    live_f = live.astype(jnp.float32)
    records = jnp.stack(
        [
            measured_datum,
            inverse_variance * live_f,
            point_of.astype(jnp.float32),
            live.astype(jnp.float32),
        ]
    )
    window = with_halo(observed, (("region", 1),), slots)
    record_window = with_halo(records, (("region", 1),), slots)
    shifts = jnp.concatenate(
        [
            jnp.full((slots,), -grid_sites, jnp.float32),
            jnp.zeros((slots,), jnp.float32),
            jnp.full((slots,), grid_sites, jnp.float32),
        ]
    )
    record_window = jnp.stack(
        [record_window[0], record_window[1], record_window[2] + shifts, record_window[3]]
    )
    gram_matrix, right_side = local_products(
        window, record_window, cutoff_distance[0].astype(jnp.float32)
    )
    weights = ensemble_weights(gram_matrix, right_side)
    extended = with_halo(weights, (("region", 0),), 1)
    return analyse(patch_tile, jnp.swapaxes(extended, 1, 2))


def solution(mesh):
    return jax.shard_map(
        local,
        mesh=mesh,
        in_specs=(
            P("region", "level", None),
            P("region"),
            P("region"),
            P("region"),
            P("region"),
            P("region"),
        ),
        out_specs=P("region", "level", None),
        check_vma=False,
    )
```

```python
import itertools

import jax
import jax.numpy as jnp
from jax import lax
from jax.experimental import pallas as pl
from jax.experimental.pallas import tpu as pltpu
from jax.sharding import PartitionSpec as P

COARSE = 6
SPACING = 256
NS_ITERS = 5


inflation = 1.1

MESH = pl.DeviceIdType.MESH
GROUP = 64
OWN = 4
MEMBERS = OWN * GROUP
LEVELS = 8
CELLS = COARSE * SPACING
HALF = SPACING // 2
HALVES = CELLS // HALF
SLOTS = 512
LANES = 128
RUNS = SLOTS // LANES
PACK = 11
PIECES_IN = 3
PIECES_OUT = 6
FIRST = 40
LATER = 15
BETWEEN = 12

SITES, PICKED, PART, PRIOR, ANALYSIS, RECORD, HALO, EDGE = 0, 1, 2, 3, 4, 5, 7, 9
KINDS = 11


def link_load(offset):
    dz, dy, dx, _ = offset
    return [float(dx in (1, 2)), float(dx in (3, 2)), float(dz in (1, 2)), float(dz in (3, 2)), float(dy)]


def balanced_order():
    left = [o for o in itertools.product(range(4), range(2), range(4), range(2)) if any(o)]
    total, order = [0.0] * 5, []
    while left:
        best = None
        for offset in left:
            after = [0.8 * a + b for a, b in zip(total, link_load(offset))]
            middle = sum(after) / 5
            score = sum((v - middle) ** 2 for v in after) - 0.3 * sum(link_load(offset))
            if best is None or score < best[0] - 1e-9:
                best = (score, offset, after)
        order.append(best[1])
        left.remove(best[1])
        total = best[2]
    return order


def peer_at(me, offset):
    core, x, y, z = me % 2, me // 2 % 4, me // 8 % 2, me // 16
    sign = 1 - 2 * core
    dz, dy, dx, dc = offset
    z, y = (z + sign * dz + 4) % 4, (y + dy) % 2
    x, core = (x + sign * dx + 4) % 4, (core + dc) % 2
    return ((z * 2 + y) * 4 + x) * 2 + core


def gather_region(region, level, own, sites, picked):
    codes = [jnp.broadcast_to(sites[region, run : run + 1, :], (LEVELS, LANES)) for run in range(RUNS)]
    cell = [code & (2**PACK - 1) for code in codes]
    lane = [c & (LANES - 1) for c in cell]
    tile = [c >> 7 for c in cell]
    tier = lax.broadcasted_iota(jnp.int32, (LEVELS, LANES), 0) + level * LEVELS
    here = [(code >> PACK) == tier for code in codes]
    rows = []
    for member in range(OWN):
        found = [jnp.zeros((LEVELS, LANES), jnp.float32)] * RUNS
        for column in range(CELLS // LANES):
            at = pl.multiple_of(region * CELLS + column * LANES, LANES)
            field = own[member, :, pl.ds(at, LANES)].astype(jnp.float32)
            for run in range(RUNS):
                taken = jnp.take_along_axis(field, lane[run], axis=1, mode="promise_in_bounds")
                found[run] = jnp.where(tile[run] == column, taken, found[run])
        for run in range(RUNS):
            rows.append(jnp.sum(jnp.where(here[run], found[run], 0.0), axis=0, keepdims=True))
    picked[region] = jnp.concatenate(rows, axis=0).astype(jnp.bfloat16)


def in_line(rows):
    return jnp.concatenate([rows[i : i + 1, :] for i in range(RUNS)], axis=1)


def halves(value):
    high = value.astype(jnp.bfloat16)
    return high, (value - high.astype(jnp.float32)).astype(jnp.bfloat16)


def product(left, right):
    (lh, ll), (rh, rl) = left, right
    return (
        jnp.dot(lh, rh, preferred_element_type=jnp.float32)
        + jnp.dot(lh, rl, preferred_element_type=jnp.float32)
        + jnp.dot(ll, rh, preferred_element_type=jnp.float32)
    )


def row_product(row, matrix):
    dims = (((1,), (1,)), ((), ()))
    (lh, ll), (rh, rl) = halves(row), matrix
    return (
        lax.dot_general(lh, rh, dims, preferred_element_type=jnp.float32)
        + lax.dot_general(lh, rl, dims, preferred_element_type=jnp.float32)
        + lax.dot_general(ll, rh, dims, preferred_element_type=jnp.float32)
    )


def window_products(window, sites, records, radius, me, departure, lines, gram, right_side):
    for part in range(3):
        columns = slice(part * SLOTS, (part + 1) * SLOTS)
        code = in_line(sites[lax.rem(me + part + GROUP - 1, GROUP)])
        both = records[part]
        datum, inverse = in_line(both), in_line(both[RUNS:, :])
        values = window[part].astype(jnp.float32)
        centre = jnp.sum(values, axis=0, keepdims=True) * (1.0 / MEMBERS)
        departure[:, columns] = values - centre
        lines[0:1, columns] = jnp.where(code >= 0, datum - centre, 0.0)
        lines[1:2, columns] = ((code & (2**PACK - 1)) + (part - 1) * CELLS).astype(jnp.float32)
        lines[2:3, columns] = inverse

    @pl.loop(0, COARSE)
    def _(point):
        spot = (HALF + SPACING * point).astype(jnp.float32)
        distance = (lines[1:2, :] - spot) / radius
        root = jnp.sqrt(jnp.exp(-0.5 * distance * distance) * lines[2:3, :])
        weighted = jnp.broadcast_to(root * lines[0:1, :], (16, 3 * SLOTS)).astype(jnp.bfloat16)
        scaled = (departure[...] * root).astype(jnp.bfloat16)
        dims = (((1,), (1,)), ((), ()))
        gram[point] = lax.dot_general(scaled, scaled, dims, preferred_element_type=jnp.float32)
        right_side[point] = lax.dot_general(weighted, scaled, dims, preferred_element_type=jnp.float32)


def ensemble_weights(points, gram, right_side, mixing):
    same = lax.broadcasted_iota(jnp.int32, (MEMBERS, MEMBERS), 0) == lax.broadcasted_iota(
        jnp.int32, (MEMBERS, MEMBERS), 1
    )
    identity = jnp.where(same, 1.0, 0.0)
    iterates, factors, inverses, norms = {}, {}, {}, {}
    for p in points:
        shifted = gram[p] + identity * ((MEMBERS - 1) / inflation)
        square = jnp.sum(jnp.sum(shifted * shifted, axis=0, keepdims=True), axis=1, keepdims=True)
        norms[p] = jnp.sqrt(square)
        iterates[p] = shifted / norms[p]
        factors[p] = 1.5 * identity - 0.5 * iterates[p]
        inverses[p] = halves(factors[p])
        iterates[p] = product(halves(iterates[p]), inverses[p])
    for turn in range(1, NS_ITERS):
        for p in points:
            held = halves(iterates[p])
            factor = halves(1.5 * identity - 0.5 * product(inverses[p], held))
            if turn < NS_ITERS - 1:
                iterates[p] = product(held, factor)
            inverses[p] = product(factor, inverses[p])
            if turn < NS_ITERS - 1:
                inverses[p] = halves(inverses[p])
    for p in points:
        parts = halves(inverses[p])
        centre = row_product(row_product(right_side[p], parts), parts)[0:1, :] / norms[p]
        weights = inverses[p] * jnp.sqrt((MEMBERS - 1.0) / norms[p]) + centre
        mean = jnp.sum(weights, axis=1, keepdims=True) * (1.0 / MEMBERS)
        mixing[p + 1] = (weights - mean + 1.0 / MEMBERS).astype(jnp.bfloat16)


def analyse_half(half, patch, mixing, result, wide_in, wide_out):
    members = OWN * GROUP
    at = pl.multiple_of(half * HALF, HALF)
    wide_in[...] = patch[:, :, pl.ds(at, HALF)].astype(jnp.float32).reshape(members * LEVELS, HALF)
    first = (half + 1) // 2
    low, high = mixing[first], mixing[first + 1]
    lane = lax.broadcasted_iota(jnp.int32, (1, HALF), 1)
    frac = (lane + jnp.where(half % 2 == 0, HALF, 0)).astype(jnp.float32) / SPACING
    frac = jnp.concatenate([frac, frac], axis=1)
    for tier in range(0, LEVELS, 2):
        field = jnp.concatenate(
            [wide_in[pl.ds(tier + t, members, stride=LEVELS), :] for t in range(2)], axis=1
        ).astype(jnp.bfloat16)
        before = jnp.dot(low, field, preferred_element_type=jnp.float32)
        beyond = jnp.dot(high, field, preferred_element_type=jnp.float32)
        mixed = (1.0 - frac) * before + frac * beyond
        for t in range(2):
            wide_out[pl.ds(tier + t, members, stride=LEVELS), :] = mixed[:, t * HALF : (t + 1) * HALF]
    result[:, :, pl.ds(at, HALF)] = wide_out[...].reshape(members, LEVELS, HALF).astype(jnp.bfloat16)


def encode(site_ref, datum_ref, inverse_ref, active, codes, records):
    site = site_ref[...]
    row = lax.broadcasted_iota(jnp.int32, (RUNS, LANES), 0)
    live = row * LANES + lax.broadcasted_iota(jnp.int32, (RUNS, LANES), 1) < active
    tier = jnp.zeros((RUNS, LANES), jnp.int32)
    for bound in range(1, 2 * LEVELS):
        tier += (site >= bound * CELLS).astype(jnp.int32)
    code = jnp.where(live, tier * 2**PACK + (site - tier * CELLS), -1)
    codes[...] = jnp.concatenate([code, code], axis=0)
    inverse = jnp.where(live, inverse_ref[...], 0.0)
    records[...] = jnp.concatenate([datum_ref[...], inverse], axis=0)


def cycle_kernel(
    site_ref,
    datum_ref,
    inverse_ref,
    active_ref,
    cutoff_ref,
    prior,
    out,
    own,
    patch,
    result,
    codes,
    my_codes,
    records,
    picked,
    arrived,
    lines,
    part_own,
    part_peer,
    window,
    departure,
    columns,
    gram,
    right_side,
    mixing,
    wide_in,
    wide_out,
    send,
    recv,
    near,
):
    me, level = lax.axis_index("region"), lax.axis_index("level")
    left, right = lax.rem(me + GROUP - 1, GROUP), lax.rem(me + 1, GROUP)
    my_cells = pl.multiple_of(me * CELLS, CELLS)
    order = balanced_order()

    def remote(kind, source, target, peer, tier=level):
        return pltpu.make_async_remote_copy(
            src_ref=source,
            dst_ref=target,
            send_sem=send.at[kind],
            recv_sem=recv.at[kind],
            device_id=(peer, tier),
            device_id_type=MESH,
        )

    def await_bytes(ref, sem):
        pltpu.make_async_copy(ref, ref, sem).wait()

    load_own = pltpu.make_async_copy(prior, own, near.at[0])
    load_own.start()
    load_mine = pltpu.make_async_copy(
        prior.at[:, :, pl.ds(my_cells, CELLS)], patch.at[pl.ds(OWN * me, OWN)], near.at[1]
    )
    load_mine.start()

    barrier = pltpu.get_barrier_semaphore()
    pl.semaphore_signal(barrier, inc=1, device_id=(me, 1 - level), device_id_type=MESH)

    @pl.loop(1, GROUP)
    def _(step):
        pl.semaphore_signal(barrier, inc=1, device_id=(lax.rem(me + step, GROUP), level), device_id_type=MESH)

    encode(site_ref, datum_ref, inverse_ref, active_ref[0], my_codes, records.at[1])
    codes[me] = my_codes[...]
    pl.semaphore_wait(barrier, GROUP)

    @pl.loop(1, GROUP)
    def _(step):
        remote(SITES, my_codes, codes.at[me], lax.rem(me + step, GROUP)).start()

    to_right = [remote(RECORD, records.at[1], records.at[0], right)]
    to_left = [remote(RECORD + 1, records.at[1], records.at[2], left)]
    to_right[0].start()
    to_left[0].start()

    width_in = CELLS // PIECES_IN
    messages = [(piece, offset) for piece in range(PIECES_IN) for offset in order]

    def issue(first, last):
        for piece, offset in messages[first:last]:
            peer = peer_at(me, offset)
            at = pl.multiple_of(peer * CELLS + piece * width_in, width_in)
            remote(
                PRIOR,
                prior.at[:, :, pl.ds(at, width_in)],
                patch.at[pl.ds(OWN * me, OWN), :, pl.ds(piece * width_in, width_in)],
                peer,
            ).start()

    issued = FIRST
    issue(0, issued)
    load_own.wait()
    await_bytes(codes.at[pl.ds(0, GROUP - 1)], recv.at[SITES])
    for quarter in range(4):

        @pl.loop(quarter * GROUP // 4, (quarter + 1) * GROUP // 4)
        def _(region):
            gather_region(region, level, own, codes, picked)

        if quarter < 3:
            issue(issued, issued + LATER)
            issued += LATER

    @pl.loop(1, GROUP)
    def _(step):
        peer = lax.rem(me + step, GROUP)
        remote(PICKED, picked.at[peer], arrived.at[me], peer).start()

    issue(issued, issued + BETWEEN)
    issued += BETWEEN
    arrived[me] = picked[me]
    await_bytes(arrived.at[pl.ds(0, GROUP - 1)], recv.at[PICKED])
    lines[...] = arrived[...].astype(jnp.float32).reshape(MEMBERS * RUNS, LANES)
    part_own[...] = jnp.concatenate(
        [lines[pl.ds(run, MEMBERS, stride=RUNS), :] for run in range(RUNS)], axis=1
    ).astype(jnp.bfloat16)
    across = remote(PART, part_own, part_peer, me, 1 - level)
    across.start()
    issue(issued, issued + BETWEEN)
    issued += BETWEEN
    across.wait_recv()
    window[1] = (part_own[...].astype(jnp.float32) + part_peer[...].astype(jnp.float32)).astype(jnp.bfloat16)
    to_right.append(remote(HALO, window.at[1], window.at[0], right))
    to_left.append(remote(HALO + 1, window.at[1], window.at[2], left))
    to_right[1].start()
    to_left[1].start()
    issue(issued, issued + BETWEEN)
    issued += BETWEEN
    for copy in to_right + to_left:
        copy.wait_recv()
    issue(issued, len(messages))

    radius = cutoff_ref[0].astype(jnp.float32)
    window_products(window, codes, records, radius, me, departure, columns, gram, right_side)
    ensemble_weights((0, COARSE - 1), gram, right_side, mixing)
    to_right.append(remote(EDGE, mixing.at[COARSE], mixing.at[0], right))
    to_left.append(remote(EDGE + 1, mixing.at[1], mixing.at[COARSE + 1], left))
    to_right[2].start()
    to_left[2].start()
    ensemble_weights((1, 2), gram, right_side, mixing)
    ensemble_weights((3, 4), gram, right_side, mixing)
    to_right[2].wait_recv()
    to_left[2].wait_recv()
    load_mine.wait()
    others = patch.at[pl.ds(0, OWN * (GROUP - 1))]
    await_bytes(others, recv.at[PRIOR])

    per_piece = HALVES // PIECES_OUT
    width = CELLS // PIECES_OUT

    @pl.loop(0, PIECES_OUT)
    def _(piece):
        @pl.loop(0, per_piece)
        def _(step):
            analyse_half(piece * per_piece + step, patch, mixing, result, wide_in, wide_out)

        at = pl.multiple_of(piece * width, width)
        for offset in order:
            peer = peer_at(me, offset)
            remote(
                ANALYSIS,
                result.at[pl.ds(OWN * peer, OWN), :, pl.ds(at, width)],
                out.at[:, :, pl.ds(pl.multiple_of(my_cells + at, width), width)],
                peer,
            ).start()

    store_mine = pltpu.make_async_copy(
        result.at[pl.ds(OWN * me, OWN)], out.at[:, :, pl.ds(my_cells, CELLS)], near.at[2]
    )
    store_mine.start()
    await_bytes(codes.at[pl.ds(0, GROUP - 1)], send.at[SITES])
    await_bytes(arrived.at[pl.ds(0, GROUP - 1)], send.at[PICKED])
    across.wait_send()
    for copy in to_right + to_left:
        copy.wait_send()
    await_bytes(others, send.at[PRIOR])
    store_mine.wait()
    await_bytes(others, recv.at[ANALYSIS])
    await_bytes(others, send.at[ANALYSIS])


def local(
    prior_samples, measured_site, measured_datum, inverse_variance, active_slots, cutoff_distance
):
    vmem = pl.BlockSpec(memory_space=pltpu.VMEM)
    smem = pl.BlockSpec(memory_space=pltpu.SMEM)
    hbm = pl.BlockSpec(memory_space=pl.ANY)
    block = (MEMBERS, LEVELS, CELLS)
    return pl.pallas_call(
        cycle_kernel,
        out_shape=jax.ShapeDtypeStruct(prior_samples.shape, jnp.bfloat16),
        in_specs=[vmem, vmem, vmem, smem, smem, hbm],
        out_specs=hbm,
        scratch_shapes=[
            pltpu.VMEM(prior_samples.shape, jnp.bfloat16),
            pltpu.VMEM(block, jnp.bfloat16),
            pltpu.VMEM(block, jnp.bfloat16),
            pltpu.VMEM((GROUP, 2 * RUNS, LANES), jnp.int32),
            pltpu.VMEM((2 * RUNS, LANES), jnp.int32),
            pltpu.VMEM((3, 2 * RUNS, LANES), jnp.float32),
            pltpu.VMEM((GROUP, OWN * RUNS, LANES), jnp.bfloat16),
            pltpu.VMEM((GROUP, OWN * RUNS, LANES), jnp.bfloat16),
            pltpu.VMEM((MEMBERS * RUNS, LANES), jnp.float32),
            pltpu.VMEM((MEMBERS, SLOTS), jnp.bfloat16),
            pltpu.VMEM((MEMBERS, SLOTS), jnp.bfloat16),
            pltpu.VMEM((3, MEMBERS, SLOTS), jnp.bfloat16),
            pltpu.VMEM((MEMBERS, 3 * SLOTS), jnp.float32),
            pltpu.VMEM((8, 3 * SLOTS), jnp.float32),
            pltpu.VMEM((COARSE, MEMBERS, MEMBERS), jnp.float32),
            pltpu.VMEM((COARSE, 16, MEMBERS), jnp.float32),
            pltpu.VMEM((COARSE + 2, MEMBERS, MEMBERS), jnp.bfloat16),
            pltpu.VMEM((MEMBERS * LEVELS, HALF), jnp.float32),
            pltpu.VMEM((MEMBERS * LEVELS, HALF), jnp.float32),
            pltpu.SemaphoreType.DMA((KINDS,)),
            pltpu.SemaphoreType.DMA((KINDS,)),
            pltpu.SemaphoreType.DMA((3,)),
        ],
        compiler_params=pltpu.CompilerParams(
            collective_id=0, has_side_effects=True, vmem_limit_bytes=48 * 2**20
        ),
    )(
        measured_site.reshape(RUNS, LANES),
        measured_datum.reshape(RUNS, LANES),
        inverse_variance.reshape(RUNS, LANES),
        active_slots,
        cutoff_distance,
        prior_samples,
    )


def solution(mesh):
    return jax.shard_map(
        local,
        mesh=mesh,
        in_specs=(
            P("region", "level", None),
            P("region"),
            P("region"),
            P("region"),
            P("region"),
            P("region"),
        ),
        out_specs=P("region", "level", None),
        check_vma=False,
    )
```

```python
import itertools

import jax
import jax.numpy as jnp
from jax import lax
from jax.experimental import pallas as pl
from jax.experimental.pallas import tpu as pltpu
from jax.sharding import PartitionSpec as P

COARSE = 6
SPACING = 256
NS_ITERS = 5


inflation = 1.1

MESH = pl.DeviceIdType.MESH
GROUP = 64
OWN = 4
MEMBERS = OWN * GROUP
LEVELS = 8
CELLS = COARSE * SPACING
HALF = SPACING // 2
HALVES = CELLS // HALF
SLOTS = 512
LANES = 128
RUNS = SLOTS // LANES
PACK = 11
PIECES_IN = 3
PIECES_OUT = 6
FIRST = 40
LATER = 15
BETWEEN = 8
BLOCKS = 8
AMONG_PARTS = 2
AMONG_HALOS = 2

SITES, PICKED, PRIOR, ANALYSIS, RECORD, HALO, EDGE = 0, 1, 2, 3, 4, 6, 8
KINDS = 10


def link_load(offset):
    dz, dy, dx, _ = offset
    return [float(dx in (1, 2)), float(dx in (3, 2)), float(dz in (1, 2)), float(dz in (3, 2)), float(dy)]


def balanced_order():
    left = [o for o in itertools.product(range(4), range(2), range(4), range(2)) if any(o)]
    total, order = [0.0] * 5, []
    while left:
        best = None
        for offset in left:
            after = [0.8 * a + b for a, b in zip(total, link_load(offset))]
            middle = sum(after) / 5
            score = sum((v - middle) ** 2 for v in after) - 0.3 * sum(link_load(offset))
            if best is None or score < best[0] - 1e-9:
                best = (score, offset, after)
        order.append(best[1])
        left.remove(best[1])
        total = best[2]
    return order


def peer_at(me, offset):
    core, x, y, z = me % 2, me // 2 % 4, me // 8 % 2, me // 16
    sign = 1 - 2 * core
    dz, dy, dx, dc = offset
    z, y = (z + sign * dz + 4) % 4, (y + dy) % 2
    x, core = (x + sign * dx + 4) % 4, (core + dc) % 2
    return ((z * 2 + y) * 4 + x) * 2 + core


def gather_region(region, level, own, sites, picked):
    codes = [jnp.broadcast_to(sites[region, run : run + 1, :], (LEVELS, LANES)) for run in range(RUNS)]
    cell = [code & (2**PACK - 1) for code in codes]
    lane = [c & (LANES - 1) for c in cell]
    tile = [c >> 7 for c in cell]
    tier = lax.broadcasted_iota(jnp.int32, (LEVELS, LANES), 0) + level * LEVELS
    here = [(code >> PACK) == tier for code in codes]
    rows = []
    for member in range(OWN):
        found = [jnp.zeros((LEVELS, LANES), jnp.float32)] * RUNS
        for column in range(CELLS // LANES):
            at = pl.multiple_of(region * CELLS + column * LANES, LANES)
            field = own[member, :, pl.ds(at, LANES)].astype(jnp.float32)
            for run in range(RUNS):
                taken = jnp.take_along_axis(field, lane[run], axis=1, mode="promise_in_bounds")
                found[run] = jnp.where(tile[run] == column, taken, found[run])
        for run in range(RUNS):
            rows.append(jnp.sum(jnp.where(here[run], found[run], 0.0), axis=0, keepdims=True))
    picked[region] = jnp.concatenate(rows, axis=0).astype(jnp.bfloat16)


def in_line(rows):
    return jnp.concatenate([rows[i : i + 1, :] for i in range(RUNS)], axis=1)


def thirds(value):
    high = value.astype(jnp.bfloat16)
    rest = value - high.astype(jnp.float32)
    middle = rest.astype(jnp.bfloat16)
    return high, middle, (rest - middle.astype(jnp.float32)).astype(jnp.bfloat16)


def product(left, right, contract=0):
    dims = (((1,), (contract,)), ((), ()))

    def term(a, b):
        return lax.dot_general(left[a], right[b], dims, preferred_element_type=jnp.float32)

    small = term(0, 2) + term(1, 1) + term(2, 0)
    return term(0, 0) + (term(0, 1) + term(1, 0) + small)


def row_product(row, matrix):
    return product(thirds(row), matrix, 1)


def window_products(window, sites, records, radius, me, departure, lines, gram, right_side):
    for part in range(3):
        columns = slice(part * SLOTS, (part + 1) * SLOTS)
        code = in_line(sites[lax.rem(me + part + GROUP - 1, GROUP)])
        both = records[part]
        datum, inverse = in_line(both), in_line(both[RUNS:, :])
        values = window[part].astype(jnp.float32)
        centre = jnp.sum(values, axis=0, keepdims=True) * (1.0 / MEMBERS)
        departure[:, columns] = values - centre
        lines[0:1, columns] = jnp.where(code >= 0, datum - centre, 0.0)
        lines[1:2, columns] = ((code & (2**PACK - 1)) + (part - 1) * CELLS).astype(jnp.float32)
        lines[2:3, columns] = inverse

    @pl.loop(0, COARSE)
    def _(point):
        spot = (HALF + SPACING * point).astype(jnp.float32)
        distance = (lines[1:2, :] - spot) / radius
        root = jnp.sqrt(jnp.exp(-0.5 * distance * distance) * lines[2:3, :])
        weighted = jnp.broadcast_to(root * lines[0:1, :], (16, 3 * SLOTS)).astype(jnp.bfloat16)
        scaled = (departure[...] * root).astype(jnp.bfloat16)
        dims = (((1,), (1,)), ((), ()))
        gram[point] = lax.dot_general(scaled, scaled, dims, preferred_element_type=jnp.float32)
        right_side[point] = lax.dot_general(weighted, scaled, dims, preferred_element_type=jnp.float32)


def ensemble_weights(points, gram, right_side, mixing):
    same = lax.broadcasted_iota(jnp.int32, (MEMBERS, MEMBERS), 0) == lax.broadcasted_iota(
        jnp.int32, (MEMBERS, MEMBERS), 1
    )
    identity = jnp.where(same, 1.0, 0.0)
    iterates, factors, inverses, norms = {}, {}, {}, {}
    for p in points:
        shifted = gram[p] + identity * ((MEMBERS - 1) / inflation)
        square = jnp.sum(jnp.sum(shifted * shifted, axis=0, keepdims=True), axis=1, keepdims=True)
        norms[p] = jnp.sqrt(square)
        iterates[p] = shifted / norms[p]
        factors[p] = 1.5 * identity - 0.5 * iterates[p]
        inverses[p] = thirds(factors[p])
        iterates[p] = product(thirds(iterates[p]), inverses[p])
    for turn in range(1, NS_ITERS):
        for p in points:
            held = thirds(iterates[p])
            factor = thirds(1.5 * identity - 0.5 * product(inverses[p], held))
            if turn < NS_ITERS - 1:
                iterates[p] = product(held, factor)
            inverses[p] = product(factor, inverses[p])
            if turn < NS_ITERS - 1:
                inverses[p] = thirds(inverses[p])
    for p in points:
        parts = thirds(inverses[p])
        centre = row_product(row_product(right_side[p], parts), parts)[0:1, :] / norms[p]
        weights = inverses[p] * jnp.sqrt((MEMBERS - 1.0) / norms[p]) + centre
        mean = jnp.sum(weights, axis=1, keepdims=True) * (1.0 / MEMBERS)
        mixing[p + 1] = (weights - mean + 1.0 / MEMBERS).astype(jnp.bfloat16)


def analyse_half(half, patch, mixing, result, wide_in, wide_out):
    members = OWN * GROUP
    at = pl.multiple_of(half * HALF, HALF)
    wide_in[...] = patch[:, :, pl.ds(at, HALF)].astype(jnp.float32).reshape(members * LEVELS, HALF)
    first = (half + 1) // 2
    low, high = mixing[first], mixing[first + 1]
    lane = lax.broadcasted_iota(jnp.int32, (1, HALF), 1)
    frac = (lane + jnp.where(half % 2 == 0, HALF, 0)).astype(jnp.float32) / SPACING
    frac = jnp.concatenate([frac, frac], axis=1)
    for tier in range(0, LEVELS, 2):
        field = jnp.concatenate(
            [wide_in[pl.ds(tier + t, members, stride=LEVELS), :] for t in range(2)], axis=1
        ).astype(jnp.bfloat16)
        before = jnp.dot(low, field, preferred_element_type=jnp.float32)
        beyond = jnp.dot(high, field, preferred_element_type=jnp.float32)
        mixed = (1.0 - frac) * before + frac * beyond
        for t in range(2):
            wide_out[pl.ds(tier + t, members, stride=LEVELS), :] = mixed[:, t * HALF : (t + 1) * HALF]
    result[:, :, pl.ds(at, HALF)] = wide_out[...].reshape(members, LEVELS, HALF).astype(jnp.bfloat16)


def encode(facts, active, codes, records):
    site = facts[0:RUNS, :].astype(jnp.int32)
    row = lax.broadcasted_iota(jnp.int32, (RUNS, LANES), 0)
    live = row * LANES + lax.broadcasted_iota(jnp.int32, (RUNS, LANES), 1) < active
    tier = jnp.zeros((RUNS, LANES), jnp.int32)
    for bound in range(1, 2 * LEVELS):
        tier += (site >= bound * CELLS).astype(jnp.int32)
    code = jnp.where(live, tier * 2**PACK + (site - tier * CELLS), -1)
    codes[...] = code
    inverse = jnp.where(live, facts[2 * RUNS : 3 * RUNS, :], 0.0)
    records[...] = jnp.concatenate([facts[RUNS : 2 * RUNS, :], inverse], axis=0)


def cycle_kernel(
    facts,
    active_ref,
    cutoff_ref,
    prior,
    out,
    own,
    patch,
    result,
    codes,
    my_codes,
    records,
    picked,
    arrived,
    lines,
    part_own,
    part_peer,
    window,
    departure,
    columns,
    gram,
    right_side,
    mixing,
    wide_in,
    wide_out,
    send,
    recv,
    part_send,
    part_recv,
    near,
):
    me, level = lax.axis_index("region"), lax.axis_index("level")
    left, right = lax.rem(me + GROUP - 1, GROUP), lax.rem(me + 1, GROUP)
    my_cells = pl.multiple_of(me * CELLS, CELLS)
    order = balanced_order()

    def remote(kind, source, target, peer, tier=level):
        return pltpu.make_async_remote_copy(
            src_ref=source,
            dst_ref=target,
            send_sem=send.at[kind],
            recv_sem=recv.at[kind],
            device_id=(peer, tier),
            device_id_type=MESH,
        )

    def await_bytes(ref, sem):
        pltpu.make_async_copy(ref, ref, sem).wait()

    load_own = pltpu.make_async_copy(prior, own, near.at[0])
    load_own.start()
    load_mine = pltpu.make_async_copy(
        prior.at[:, :, pl.ds(my_cells, CELLS)], patch.at[pl.ds(OWN * me, OWN)], near.at[1]
    )
    load_mine.start()

    barrier = pltpu.get_barrier_semaphore()
    pl.semaphore_signal(barrier, inc=1, device_id=(me, 1 - level), device_id_type=MESH)

    @pl.loop(1, GROUP)
    def _(step):
        pl.semaphore_signal(barrier, inc=1, device_id=(lax.rem(me + step, GROUP), level), device_id_type=MESH)

    encode(facts, active_ref[0], my_codes, records.at[1])
    codes[me, 0:RUNS] = my_codes[...]
    pl.semaphore_wait(barrier, GROUP)

    for offset in order:
        remote(SITES, my_codes, codes.at[me, 0:RUNS], peer_at(me, offset)).start()

    to_right = [remote(RECORD, records.at[1], records.at[0], right)]
    to_left = [remote(RECORD + 1, records.at[1], records.at[2], left)]
    to_right[0].start()
    to_left[0].start()

    width_in = CELLS // PIECES_IN
    messages = [(piece, offset) for piece in range(PIECES_IN) for offset in order]

    def issue(first, last):
        for piece, offset in messages[first:last]:
            peer = peer_at(me, offset)
            at = pl.multiple_of(peer * CELLS + piece * width_in, width_in)
            remote(
                PRIOR,
                prior.at[:, :, pl.ds(at, width_in)],
                patch.at[pl.ds(OWN * me, OWN), :, pl.ds(piece * width_in, width_in)],
                peer,
            ).start()

    issued = FIRST
    issue(0, issued)
    load_own.wait()
    await_bytes(codes.at[pl.ds(0, GROUP - 1), 0:RUNS], recv.at[SITES])
    for quarter in range(4):

        @pl.loop(quarter * GROUP // 4, (quarter + 1) * GROUP // 4)
        def _(region):
            gather_region(region, level, own, codes, picked)

        if quarter < 3:
            issue(issued, issued + LATER)
            issued += LATER

    for offset in order:
        peer = peer_at(me, offset)
        remote(PICKED, picked.at[peer], arrived.at[me], peer).start()

    issue(issued, issued + BETWEEN)
    issued += BETWEEN
    arrived[me] = picked[me]
    await_bytes(arrived.at[pl.ds(0, GROUP - 1)], recv.at[PICKED])
    lines[...] = arrived[...].astype(jnp.float32).reshape(MEMBERS * RUNS, LANES)
    part_own[...] = jnp.concatenate(
        [lines[pl.ds(run, MEMBERS, stride=RUNS), :] for run in range(RUNS)], axis=1
    ).astype(jnp.bfloat16)
    tall = MEMBERS // BLOCKS
    across = []
    for block in range(BLOCKS):
        rows = slice(block * tall, (block + 1) * tall)
        across.append(
            pltpu.make_async_remote_copy(
                src_ref=part_own.at[rows],
                dst_ref=part_peer.at[rows],
                send_sem=part_send.at[block],
                recv_sem=part_recv.at[block],
                device_id=(me, 1 - level),
                device_id_type=MESH,
            )
        )
        across[block].start()
        issue(issued, issued + AMONG_PARTS)
        issued += AMONG_PARTS
    for block in range(BLOCKS):
        rows = slice(block * tall, (block + 1) * tall)
        across[block].wait_recv()
        window[1, rows] = (
            part_own[rows, :].astype(jnp.float32) + part_peer[rows, :].astype(jnp.float32)
        ).astype(jnp.bfloat16)
        remote(HALO, window.at[1, rows], window.at[0, rows], right).start()
        remote(HALO + 1, window.at[1, rows], window.at[2, rows], left).start()
        issue(issued, issued + AMONG_HALOS)
        issued += AMONG_HALOS
    to_right.append(remote(HALO, window.at[1], window.at[0], right))
    to_left.append(remote(HALO + 1, window.at[1], window.at[2], left))
    for copy in to_right + to_left:
        copy.wait_recv()
    issue(issued, len(messages))

    radius = cutoff_ref[0].astype(jnp.float32)
    window_products(window, codes, records, radius, me, departure, columns, gram, right_side)
    ensemble_weights((0, COARSE - 1), gram, right_side, mixing)
    to_right.append(remote(EDGE, mixing.at[COARSE], mixing.at[0], right))
    to_left.append(remote(EDGE + 1, mixing.at[1], mixing.at[COARSE + 1], left))
    to_right[2].start()
    to_left[2].start()
    ensemble_weights((1, 2), gram, right_side, mixing)
    ensemble_weights((3, 4), gram, right_side, mixing)
    to_right[2].wait_recv()
    to_left[2].wait_recv()
    load_mine.wait()
    others = patch.at[pl.ds(0, OWN * (GROUP - 1))]
    await_bytes(others, recv.at[PRIOR])

    per_piece = HALVES // PIECES_OUT
    width = CELLS // PIECES_OUT

    @pl.loop(0, PIECES_OUT)
    def _(piece):
        @pl.loop(0, per_piece)
        def _(step):
            analyse_half(piece * per_piece + step, patch, mixing, result, wide_in, wide_out)

        at = pl.multiple_of(piece * width, width)
        for offset in order:
            peer = peer_at(me, offset)
            remote(
                ANALYSIS,
                result.at[pl.ds(OWN * peer, OWN), :, pl.ds(at, width)],
                out.at[:, :, pl.ds(pl.multiple_of(my_cells + at, width), width)],
                peer,
            ).start()

    store_mine = pltpu.make_async_copy(
        result.at[pl.ds(OWN * me, OWN)], out.at[:, :, pl.ds(my_cells, CELLS)], near.at[2]
    )
    store_mine.start()
    await_bytes(codes.at[pl.ds(0, GROUP - 1), 0:RUNS], send.at[SITES])
    await_bytes(arrived.at[pl.ds(0, GROUP - 1)], send.at[PICKED])
    for copy in across:
        copy.wait_send()
    for copy in to_right + to_left:
        copy.wait_send()
    await_bytes(others, send.at[PRIOR])
    store_mine.wait()
    await_bytes(others, recv.at[ANALYSIS])
    await_bytes(others, send.at[ANALYSIS])


def local(
    prior_samples, measured_site, measured_datum, inverse_variance, active_slots, cutoff_distance
):
    vmem = pl.BlockSpec(memory_space=pltpu.VMEM)
    smem = pl.BlockSpec(memory_space=pltpu.SMEM)
    hbm = pl.BlockSpec(memory_space=pl.ANY)
    block = (MEMBERS, LEVELS, CELLS)
    return pl.pallas_call(
        cycle_kernel,
        out_shape=jax.ShapeDtypeStruct(prior_samples.shape, jnp.bfloat16),
        in_specs=[vmem, smem, smem, hbm],
        out_specs=hbm,
        scratch_shapes=[
            pltpu.VMEM(prior_samples.shape, jnp.bfloat16),
            pltpu.VMEM(block, jnp.bfloat16),
            pltpu.VMEM(block, jnp.bfloat16),
            pltpu.VMEM((GROUP, 2 * RUNS, LANES), jnp.int32),
            pltpu.VMEM((RUNS, LANES), jnp.int32),
            pltpu.VMEM((3, 2 * RUNS, LANES), jnp.float32),
            pltpu.VMEM((GROUP, OWN * RUNS, LANES), jnp.bfloat16),
            pltpu.VMEM((GROUP, OWN * RUNS, LANES), jnp.bfloat16),
            pltpu.VMEM((MEMBERS * RUNS, LANES), jnp.float32),
            pltpu.VMEM((MEMBERS, SLOTS), jnp.bfloat16),
            pltpu.VMEM((MEMBERS, SLOTS), jnp.bfloat16),
            pltpu.VMEM((3, MEMBERS, SLOTS), jnp.bfloat16),
            pltpu.VMEM((MEMBERS, 3 * SLOTS), jnp.float32),
            pltpu.VMEM((8, 3 * SLOTS), jnp.float32),
            pltpu.VMEM((COARSE, MEMBERS, MEMBERS), jnp.float32),
            pltpu.VMEM((COARSE, 16, MEMBERS), jnp.float32),
            pltpu.VMEM((COARSE + 2, MEMBERS, MEMBERS), jnp.bfloat16),
            pltpu.VMEM((MEMBERS * LEVELS, HALF), jnp.float32),
            pltpu.VMEM((MEMBERS * LEVELS, HALF), jnp.float32),
            pltpu.SemaphoreType.DMA((KINDS,)),
            pltpu.SemaphoreType.DMA((KINDS,)),
            pltpu.SemaphoreType.DMA((BLOCKS,)),
            pltpu.SemaphoreType.DMA((BLOCKS,)),
            pltpu.SemaphoreType.DMA((3,)),
        ],
        compiler_params=pltpu.CompilerParams(
            collective_id=0, has_side_effects=True, vmem_limit_bytes=44 * 2**20
        ),
    )(
        jnp.concatenate([measured_site.astype(jnp.float32), measured_datum, inverse_variance]).reshape(
            3 * RUNS, LANES
        ),
        active_slots,
        cutoff_distance,
        prior_samples,
    )


def solution(mesh):
    return jax.shard_map(
        local,
        mesh=mesh,
        in_specs=(
            P("region", "level", None),
            P("region"),
            P("region"),
            P("region"),
            P("region"),
            P("region"),
        ),
        out_specs=P("region", "level", None),
        check_vma=False,
    )
```

```python
import itertools

import jax
import jax.numpy as jnp
from jax import lax
from jax.experimental import pallas as pl
from jax.experimental.pallas import tpu as pltpu
from jax.sharding import PartitionSpec as P

COARSE = 6
SPACING = 256
NS_ITERS = 5


inflation = 1.1

MESH = pl.DeviceIdType.MESH
GROUP = 64
OWN = 4
MEMBERS = OWN * GROUP
LEVELS = 8
CELLS = COARSE * SPACING
HALF = SPACING // 2
HALVES = CELLS // HALF
SLOTS = 512
LANES = 128
RUNS = SLOTS // LANES
PACK = 11
PIECES_IN = 3
PIECES_OUT = 12
FIRST = 40
LATER = 15
BETWEEN = 8
BLOCKS = 8
AMONG_PARTS = 2
AMONG_HALOS = 2

SITES, PICKED, PRIOR, ANALYSIS, RECORD, HALO, EDGE = 0, 1, 2, 3, 4, 6, 8
KINDS = 10


def link_load(offset):
    dz, dy, dx, _ = offset
    return [float(dx in (1, 2)), float(dx in (3, 2)), float(dz in (1, 2)), float(dz in (3, 2)), float(dy)]


def balanced_order():
    left = [o for o in itertools.product(range(4), range(2), range(4), range(2)) if any(o)]
    total, order = [0.0] * 5, []
    while left:
        best = None
        for offset in left:
            after = [0.8 * a + b for a, b in zip(total, link_load(offset))]
            middle = sum(after) / 5
            score = sum((v - middle) ** 2 for v in after) - 0.3 * sum(link_load(offset))
            if best is None or score < best[0] - 1e-9:
                best = (score, offset, after)
        order.append(best[1])
        left.remove(best[1])
        total = best[2]
    return order


def peer_at(me, offset):
    core, x, y, z = me % 2, me // 2 % 4, me // 8 % 2, me // 16
    sign = 1 - 2 * core
    dz, dy, dx, dc = offset
    z, y = (z + sign * dz + 4) % 4, (y + dy) % 2
    x, core = (x + sign * dx + 4) % 4, (core + dc) % 2
    return ((z * 2 + y) * 4 + x) * 2 + core


def gather_region(region, level, own, sites, picked):
    codes = [jnp.broadcast_to(sites[region, run : run + 1, :], (LEVELS, LANES)) for run in range(RUNS)]
    cell = [code & (2**PACK - 1) for code in codes]
    lane = [c & (LANES - 1) for c in cell]
    tile = [c >> 7 for c in cell]
    tier = lax.broadcasted_iota(jnp.int32, (LEVELS, LANES), 0) + level * LEVELS
    here = [(code >> PACK) == tier for code in codes]
    rows = []
    for member in range(OWN):
        found = [jnp.zeros((LEVELS, LANES), jnp.float32)] * RUNS
        for column in range(CELLS // LANES):
            at = pl.multiple_of(region * CELLS + column * LANES, LANES)
            field = own[member, :, pl.ds(at, LANES)].astype(jnp.float32)
            for run in range(RUNS):
                taken = jnp.take_along_axis(field, lane[run], axis=1, mode="promise_in_bounds")
                found[run] = jnp.where(tile[run] == column, taken, found[run])
        for run in range(RUNS):
            rows.append(jnp.sum(jnp.where(here[run], found[run], 0.0), axis=0, keepdims=True))
    picked[region] = jnp.concatenate(rows, axis=0).astype(jnp.bfloat16)


def in_line(rows):
    return jnp.concatenate([rows[i : i + 1, :] for i in range(RUNS)], axis=1)


def thirds(value):
    high = value.astype(jnp.bfloat16)
    rest = value - high.astype(jnp.float32)
    middle = rest.astype(jnp.bfloat16)
    return high, middle, (rest - middle.astype(jnp.float32)).astype(jnp.bfloat16)


def product(left, right, contract=0):
    dims = (((1,), (contract,)), ((), ()))

    def term(a, b):
        return lax.dot_general(left[a], right[b], dims, preferred_element_type=jnp.float32)

    small = term(0, 2) + term(1, 1) + term(2, 0)
    return term(0, 0) + (term(0, 1) + term(1, 0) + small)


def row_product(row, matrix):
    return product(thirds(row), matrix, 1)


def window_products(window, sites, records, radius, me, departure, lines, gram, right_side):
    for part in range(3):
        columns = slice(part * SLOTS, (part + 1) * SLOTS)
        code = in_line(sites[lax.rem(me + part + GROUP - 1, GROUP)])
        both = records[part]
        datum, inverse = in_line(both), in_line(both[RUNS:, :])
        values = window[part].astype(jnp.float32)
        centre = jnp.sum(values, axis=0, keepdims=True) * (1.0 / MEMBERS)
        departure[:, columns] = values - centre
        lines[0:1, columns] = jnp.where(code >= 0, datum - centre, 0.0)
        lines[1:2, columns] = ((code & (2**PACK - 1)) + (part - 1) * CELLS).astype(jnp.float32)
        lines[2:3, columns] = inverse

    @pl.loop(0, COARSE)
    def _(point):
        spot = (HALF + SPACING * point).astype(jnp.float32)
        distance = (lines[1:2, :] - spot) / radius
        root = jnp.sqrt(jnp.exp(-0.5 * distance * distance) * lines[2:3, :])
        weighted = jnp.broadcast_to(root * lines[0:1, :], (16, 3 * SLOTS)).astype(jnp.bfloat16)
        scaled = (departure[...] * root).astype(jnp.bfloat16)
        dims = (((1,), (1,)), ((), ()))
        gram[point] = lax.dot_general(scaled, scaled, dims, preferred_element_type=jnp.float32)
        right_side[point] = lax.dot_general(weighted, scaled, dims, preferred_element_type=jnp.float32)


def ensemble_weights(points, gram, right_side, mixing):
    same = lax.broadcasted_iota(jnp.int32, (MEMBERS, MEMBERS), 0) == lax.broadcasted_iota(
        jnp.int32, (MEMBERS, MEMBERS), 1
    )
    identity = jnp.where(same, 1.0, 0.0)
    iterates, factors, inverses, norms = {}, {}, {}, {}
    for p in points:
        shifted = gram[p] + identity * ((MEMBERS - 1) / inflation)
        square = jnp.sum(jnp.sum(shifted * shifted, axis=0, keepdims=True), axis=1, keepdims=True)
        norms[p] = jnp.sqrt(square)
        iterates[p] = shifted / norms[p]
        factors[p] = 1.5 * identity - 0.5 * iterates[p]
        inverses[p] = thirds(factors[p])
        iterates[p] = product(thirds(iterates[p]), inverses[p])
    for turn in range(1, NS_ITERS):
        for p in points:
            held = thirds(iterates[p])
            factor = thirds(1.5 * identity - 0.5 * product(inverses[p], held))
            if turn < NS_ITERS - 1:
                iterates[p] = product(held, factor)
            inverses[p] = product(factor, inverses[p])
            if turn < NS_ITERS - 1:
                inverses[p] = thirds(inverses[p])
    for p in points:
        parts = thirds(inverses[p])
        centre = row_product(row_product(right_side[p], parts), parts)[0:1, :] / norms[p]
        weights = inverses[p] * jnp.sqrt((MEMBERS - 1.0) / norms[p]) + centre
        mean = jnp.sum(weights, axis=1, keepdims=True) * (1.0 / MEMBERS)
        mixing[p + 1] = (weights - mean + 1.0 / MEMBERS).astype(jnp.bfloat16)


def analyse_half(half, patch, mixing, result, wide_in, wide_out):
    members = OWN * GROUP
    at = pl.multiple_of(half * HALF, HALF)
    wide_in[...] = patch[:, :, pl.ds(at, HALF)].astype(jnp.float32).reshape(members * LEVELS, HALF)
    first = (half + 1) // 2
    low, high = mixing[first], mixing[first + 1]
    lane = lax.broadcasted_iota(jnp.int32, (1, HALF), 1)
    frac = (lane + jnp.where(half % 2 == 0, HALF, 0)).astype(jnp.float32) / SPACING
    frac = jnp.concatenate([frac, frac], axis=1)
    for tier in range(0, LEVELS, 2):
        field = jnp.concatenate(
            [wide_in[pl.ds(tier + t, members, stride=LEVELS), :] for t in range(2)], axis=1
        ).astype(jnp.bfloat16)
        before = jnp.dot(low, field, preferred_element_type=jnp.float32)
        beyond = jnp.dot(high, field, preferred_element_type=jnp.float32)
        mixed = (1.0 - frac) * before + frac * beyond
        for t in range(2):
            wide_out[pl.ds(tier + t, members, stride=LEVELS), :] = mixed[:, t * HALF : (t + 1) * HALF]
    result[:, :, pl.ds(at, HALF)] = wide_out[...].reshape(members, LEVELS, HALF).astype(jnp.bfloat16)


def encode(facts, active, codes, records):
    site = facts[0:RUNS, :].astype(jnp.int32)
    row = lax.broadcasted_iota(jnp.int32, (RUNS, LANES), 0)
    live = row * LANES + lax.broadcasted_iota(jnp.int32, (RUNS, LANES), 1) < active
    tier = jnp.zeros((RUNS, LANES), jnp.int32)
    for bound in range(1, 2 * LEVELS):
        tier += (site >= bound * CELLS).astype(jnp.int32)
    code = jnp.where(live, tier * 2**PACK + (site - tier * CELLS), -1)
    codes[...] = code
    inverse = jnp.where(live, facts[2 * RUNS : 3 * RUNS, :], 0.0)
    records[...] = jnp.concatenate([facts[RUNS : 2 * RUNS, :], inverse], axis=0)


def cycle_kernel(
    facts,
    active_ref,
    cutoff_ref,
    prior,
    out,
    own,
    patch,
    result,
    codes,
    my_codes,
    records,
    picked,
    arrived,
    lines,
    part_own,
    part_peer,
    window,
    departure,
    columns,
    gram,
    right_side,
    mixing,
    wide_in,
    wide_out,
    send,
    recv,
    part_send,
    part_recv,
    near,
):
    me, level = lax.axis_index("region"), lax.axis_index("level")
    left, right = lax.rem(me + GROUP - 1, GROUP), lax.rem(me + 1, GROUP)
    my_cells = pl.multiple_of(me * CELLS, CELLS)
    order = balanced_order()

    def remote(kind, source, target, peer, tier=level):
        return pltpu.make_async_remote_copy(
            src_ref=source,
            dst_ref=target,
            send_sem=send.at[kind],
            recv_sem=recv.at[kind],
            device_id=(peer, tier),
            device_id_type=MESH,
        )

    def await_bytes(ref, sem):
        pltpu.make_async_copy(ref, ref, sem).wait()

    load_own = pltpu.make_async_copy(prior, own, near.at[0])
    load_own.start()
    load_mine = pltpu.make_async_copy(
        prior.at[:, :, pl.ds(my_cells, CELLS)], patch.at[pl.ds(OWN * me, OWN)], near.at[1]
    )
    load_mine.start()

    barrier = pltpu.get_barrier_semaphore()
    pl.semaphore_signal(barrier, inc=1, device_id=(me, 1 - level), device_id_type=MESH)

    @pl.loop(1, GROUP)
    def _(step):
        pl.semaphore_signal(barrier, inc=1, device_id=(lax.rem(me + step, GROUP), level), device_id_type=MESH)

    encode(facts, active_ref[0], my_codes, records.at[1])
    codes[me, 0:RUNS] = my_codes[...]
    pl.semaphore_wait(barrier, GROUP)

    for offset in order:
        remote(SITES, my_codes, codes.at[me, 0:RUNS], peer_at(me, offset)).start()

    to_right = [remote(RECORD, records.at[1], records.at[0], right)]
    to_left = [remote(RECORD + 1, records.at[1], records.at[2], left)]
    to_right[0].start()
    to_left[0].start()

    width_in = CELLS // PIECES_IN
    messages = [(piece, offset) for piece in range(PIECES_IN) for offset in order]

    def issue(first, last):
        for piece, offset in messages[first:last]:
            peer = peer_at(me, offset)
            at = pl.multiple_of(peer * CELLS + piece * width_in, width_in)
            remote(
                PRIOR,
                prior.at[:, :, pl.ds(at, width_in)],
                patch.at[pl.ds(OWN * me, OWN), :, pl.ds(piece * width_in, width_in)],
                peer,
            ).start()

    issued = FIRST
    issue(0, issued)
    load_own.wait()
    await_bytes(codes.at[pl.ds(0, GROUP - 1), 0:RUNS], recv.at[SITES])
    for quarter in range(4):

        @pl.loop(quarter * GROUP // 4, (quarter + 1) * GROUP // 4)
        def _(region):
            gather_region(region, level, own, codes, picked)

        if quarter < 3:
            issue(issued, issued + LATER)
            issued += LATER

    for offset in order:
        peer = peer_at(me, offset)
        remote(PICKED, picked.at[peer], arrived.at[me], peer).start()

    issue(issued, issued + BETWEEN)
    issued += BETWEEN
    arrived[me] = picked[me]
    await_bytes(arrived.at[pl.ds(0, GROUP - 1)], recv.at[PICKED])
    lines[...] = arrived[...].astype(jnp.float32).reshape(MEMBERS * RUNS, LANES)
    part_own[...] = jnp.concatenate(
        [lines[pl.ds(run, MEMBERS, stride=RUNS), :] for run in range(RUNS)], axis=1
    ).astype(jnp.bfloat16)
    tall = MEMBERS // BLOCKS
    across = []
    for block in range(BLOCKS):
        rows = slice(block * tall, (block + 1) * tall)
        across.append(
            pltpu.make_async_remote_copy(
                src_ref=part_own.at[rows],
                dst_ref=part_peer.at[rows],
                send_sem=part_send.at[block],
                recv_sem=part_recv.at[block],
                device_id=(me, 1 - level),
                device_id_type=MESH,
            )
        )
        across[block].start()
        issue(issued, issued + AMONG_PARTS)
        issued += AMONG_PARTS
    for block in range(BLOCKS):
        rows = slice(block * tall, (block + 1) * tall)
        across[block].wait_recv()
        window[1, rows] = (
            part_own[rows, :].astype(jnp.float32) + part_peer[rows, :].astype(jnp.float32)
        ).astype(jnp.bfloat16)
        remote(HALO, window.at[1, rows], window.at[0, rows], right).start()
        remote(HALO + 1, window.at[1, rows], window.at[2, rows], left).start()
        issue(issued, issued + AMONG_HALOS)
        issued += AMONG_HALOS
    to_right.append(remote(HALO, window.at[1], window.at[0], right))
    to_left.append(remote(HALO + 1, window.at[1], window.at[2], left))
    for copy in to_right + to_left:
        copy.wait_recv()
    issue(issued, len(messages))

    radius = cutoff_ref[0].astype(jnp.float32)
    window_products(window, codes, records, radius, me, departure, columns, gram, right_side)
    ensemble_weights((0, COARSE - 1), gram, right_side, mixing)
    to_right.append(remote(EDGE, mixing.at[COARSE], mixing.at[0], right))
    to_left.append(remote(EDGE + 1, mixing.at[1], mixing.at[COARSE + 1], left))
    to_right[2].start()
    to_left[2].start()
    ensemble_weights((1, 2), gram, right_side, mixing)
    ensemble_weights((3, 4), gram, right_side, mixing)
    to_right[2].wait_recv()
    to_left[2].wait_recv()
    load_mine.wait()
    others = patch.at[pl.ds(0, OWN * (GROUP - 1))]
    await_bytes(others, recv.at[PRIOR])

    per_piece = HALVES // PIECES_OUT
    width = CELLS // PIECES_OUT

    @pl.loop(0, PIECES_OUT)
    def _(piece):
        @pl.loop(0, per_piece)
        def _(step):
            analyse_half(piece * per_piece + step, patch, mixing, result, wide_in, wide_out)

        at = pl.multiple_of(piece * width, width)
        for offset in order:
            peer = peer_at(me, offset)
            remote(
                ANALYSIS,
                result.at[pl.ds(OWN * peer, OWN), :, pl.ds(at, width)],
                out.at[:, :, pl.ds(pl.multiple_of(my_cells + at, width), width)],
                peer,
            ).start()

    store_mine = pltpu.make_async_copy(
        result.at[pl.ds(OWN * me, OWN)], out.at[:, :, pl.ds(my_cells, CELLS)], near.at[2]
    )
    store_mine.start()
    await_bytes(codes.at[pl.ds(0, GROUP - 1), 0:RUNS], send.at[SITES])
    await_bytes(arrived.at[pl.ds(0, GROUP - 1)], send.at[PICKED])
    for copy in across:
        copy.wait_send()
    for copy in to_right + to_left:
        copy.wait_send()
    await_bytes(others, send.at[PRIOR])
    store_mine.wait()
    await_bytes(others, recv.at[ANALYSIS])
    await_bytes(others, send.at[ANALYSIS])


def local(
    prior_samples, measured_site, measured_datum, inverse_variance, active_slots, cutoff_distance
):
    vmem = pl.BlockSpec(memory_space=pltpu.VMEM)
    smem = pl.BlockSpec(memory_space=pltpu.SMEM)
    hbm = pl.BlockSpec(memory_space=pl.ANY)
    block = (MEMBERS, LEVELS, CELLS)
    return pl.pallas_call(
        cycle_kernel,
        out_shape=jax.ShapeDtypeStruct(prior_samples.shape, jnp.bfloat16),
        in_specs=[vmem, smem, smem, hbm],
        out_specs=hbm,
        scratch_shapes=[
            pltpu.VMEM(prior_samples.shape, jnp.bfloat16),
            pltpu.VMEM(block, jnp.bfloat16),
            pltpu.VMEM(block, jnp.bfloat16),
            pltpu.VMEM((GROUP, 2 * RUNS, LANES), jnp.int32),
            pltpu.VMEM((RUNS, LANES), jnp.int32),
            pltpu.VMEM((3, 2 * RUNS, LANES), jnp.float32),
            pltpu.VMEM((GROUP, OWN * RUNS, LANES), jnp.bfloat16),
            pltpu.VMEM((GROUP, OWN * RUNS, LANES), jnp.bfloat16),
            pltpu.VMEM((MEMBERS * RUNS, LANES), jnp.float32),
            pltpu.VMEM((MEMBERS, SLOTS), jnp.bfloat16),
            pltpu.VMEM((MEMBERS, SLOTS), jnp.bfloat16),
            pltpu.VMEM((3, MEMBERS, SLOTS), jnp.bfloat16),
            pltpu.VMEM((MEMBERS, 3 * SLOTS), jnp.float32),
            pltpu.VMEM((8, 3 * SLOTS), jnp.float32),
            pltpu.VMEM((COARSE, MEMBERS, MEMBERS), jnp.float32),
            pltpu.VMEM((COARSE, 16, MEMBERS), jnp.float32),
            pltpu.VMEM((COARSE + 2, MEMBERS, MEMBERS), jnp.bfloat16),
            pltpu.VMEM((MEMBERS * LEVELS, HALF), jnp.float32),
            pltpu.VMEM((MEMBERS * LEVELS, HALF), jnp.float32),
            pltpu.SemaphoreType.DMA((KINDS,)),
            pltpu.SemaphoreType.DMA((KINDS,)),
            pltpu.SemaphoreType.DMA((BLOCKS,)),
            pltpu.SemaphoreType.DMA((BLOCKS,)),
            pltpu.SemaphoreType.DMA((3,)),
        ],
        compiler_params=pltpu.CompilerParams(
            collective_id=0, has_side_effects=True, vmem_limit_bytes=44 * 2**20
        ),
    )(
        jnp.concatenate([measured_site.astype(jnp.float32), measured_datum, inverse_variance]).reshape(
            3 * RUNS, LANES
        ),
        active_slots,
        cutoff_distance,
        prior_samples,
    )


def solution(mesh):
    return jax.shard_map(
        local,
        mesh=mesh,
        in_specs=(
            P("region", "level", None),
            P("region"),
            P("region"),
            P("region"),
            P("region"),
            P("region"),
        ),
        out_specs=P("region", "level", None),
        check_vma=False,
    )
```

```python
import itertools

import jax
import jax.numpy as jnp
from jax import lax
from jax.experimental import pallas as pl
from jax.experimental.pallas import tpu as pltpu
from jax.sharding import PartitionSpec as P

COARSE = 6
SPACING = 256
NS_ITERS = 5


inflation = 1.1

MESH = pl.DeviceIdType.MESH
GROUP = 64
OWN = 4
MEMBERS = OWN * GROUP
LEVELS = 8
CELLS = COARSE * SPACING
HALF = SPACING // 2
HALVES = CELLS // HALF
SLOTS = 512
LANES = 128
RUNS = SLOTS // LANES
PACK = 11
PIECES_IN = 3
PIECES_OUT = 12
FIRST = 40
LATER = 15
BETWEEN = 8
BLOCKS = 8
AMONG_PARTS = 2
AMONG_HALOS = 2

SITES, PICKED, ANALYSIS, RECORD, HALO, EDGE, PRIOR = 0, 1, 2, 3, 5, 7, 9
KINDS = PRIOR + PIECES_IN


def link_load(offset):
    dz, dy, dx, _ = offset
    return [float(dx in (1, 2)), float(dx in (3, 2)), float(dz in (1, 2)), float(dz in (3, 2)), float(dy)]


def balanced_order():
    left = [o for o in itertools.product(range(4), range(2), range(4), range(2)) if any(o)]
    total, order = [0.0] * 5, []
    while left:
        best = None
        for offset in left:
            after = [0.8 * a + b for a, b in zip(total, link_load(offset))]
            middle = sum(after) / 5
            score = sum((v - middle) ** 2 for v in after) - 0.3 * sum(link_load(offset))
            if best is None or score < best[0] - 1e-9:
                best = (score, offset, after)
        order.append(best[1])
        left.remove(best[1])
        total = best[2]
    return order


def peer_at(me, offset):
    core, x, y, z = me % 2, me // 2 % 4, me // 8 % 2, me // 16
    sign = 1 - 2 * core
    dz, dy, dx, dc = offset
    z, y = (z + sign * dz + 4) % 4, (y + dy) % 2
    x, core = (x + sign * dx + 4) % 4, (core + dc) % 2
    return ((z * 2 + y) * 4 + x) * 2 + core


def gather_region(region, level, own, sites, picked):
    codes = [jnp.broadcast_to(sites[region, run : run + 1, :], (LEVELS, LANES)) for run in range(RUNS)]
    cell = [code & (2**PACK - 1) for code in codes]
    lane = [c & (LANES - 1) for c in cell]
    tile = [c >> 7 for c in cell]
    tier = lax.broadcasted_iota(jnp.int32, (LEVELS, LANES), 0) + level * LEVELS
    here = [(code >> PACK) == tier for code in codes]
    rows = []
    for member in range(OWN):
        found = [jnp.zeros((LEVELS, LANES), jnp.float32)] * RUNS
        for column in range(CELLS // LANES):
            at = pl.multiple_of(region * CELLS + column * LANES, LANES)
            field = own[member, :, pl.ds(at, LANES)].astype(jnp.float32)
            for run in range(RUNS):
                taken = jnp.take_along_axis(field, lane[run], axis=1, mode="promise_in_bounds")
                found[run] = jnp.where(tile[run] == column, taken, found[run])
        for run in range(RUNS):
            rows.append(jnp.sum(jnp.where(here[run], found[run], 0.0), axis=0, keepdims=True))
    picked[region] = jnp.concatenate(rows, axis=0).astype(jnp.bfloat16)


def in_line(rows):
    return jnp.concatenate([rows[i : i + 1, :] for i in range(RUNS)], axis=1)


def thirds(value):
    high = value.astype(jnp.bfloat16)
    rest = value - high.astype(jnp.float32)
    middle = rest.astype(jnp.bfloat16)
    return high, middle, (rest - middle.astype(jnp.float32)).astype(jnp.bfloat16)


def product(left, right, contract=0):
    dims = (((1,), (contract,)), ((), ()))

    def term(a, b):
        return lax.dot_general(left[a], right[b], dims, preferred_element_type=jnp.float32)

    small = term(0, 2) + term(1, 1) + term(2, 0)
    return term(0, 0) + (term(0, 1) + term(1, 0) + small)


def row_product(row, matrix):
    return product(thirds(row), matrix, 1)


def window_products(window, sites, records, radius, me, departure, lines, gram, right_side):
    for part in range(3):
        columns = slice(part * SLOTS, (part + 1) * SLOTS)
        code = in_line(sites[lax.rem(me + part + GROUP - 1, GROUP)])
        both = records[part]
        datum, inverse = in_line(both), in_line(both[RUNS:, :])
        values = window[part].astype(jnp.float32)
        centre = jnp.sum(values, axis=0, keepdims=True) * (1.0 / MEMBERS)
        departure[:, columns] = values - centre
        lines[0:1, columns] = jnp.where(code >= 0, datum - centre, 0.0)
        lines[1:2, columns] = ((code & (2**PACK - 1)) + (part - 1) * CELLS).astype(jnp.float32)
        lines[2:3, columns] = inverse

    @pl.loop(0, COARSE)
    def _(point):
        spot = (HALF + SPACING * point).astype(jnp.float32)
        distance = (lines[1:2, :] - spot) / radius
        root = jnp.sqrt(jnp.exp(-0.5 * distance * distance) * lines[2:3, :])
        weighted = jnp.broadcast_to(root * lines[0:1, :], (16, 3 * SLOTS)).astype(jnp.bfloat16)
        scaled = (departure[...] * root).astype(jnp.bfloat16)
        dims = (((1,), (1,)), ((), ()))
        gram[point] = lax.dot_general(scaled, scaled, dims, preferred_element_type=jnp.float32)
        right_side[point] = lax.dot_general(weighted, scaled, dims, preferred_element_type=jnp.float32)


def ensemble_weights(points, gram, right_side, mixing):
    same = lax.broadcasted_iota(jnp.int32, (MEMBERS, MEMBERS), 0) == lax.broadcasted_iota(
        jnp.int32, (MEMBERS, MEMBERS), 1
    )
    identity = jnp.where(same, 1.0, 0.0)
    iterates, factors, inverses, norms = {}, {}, {}, {}
    for p in points:
        shifted = gram[p] + identity * ((MEMBERS - 1) / inflation)
        square = jnp.sum(jnp.sum(shifted * shifted, axis=0, keepdims=True), axis=1, keepdims=True)
        norms[p] = jnp.sqrt(square)
        iterates[p] = shifted / norms[p]
        factors[p] = 1.5 * identity - 0.5 * iterates[p]
        inverses[p] = thirds(factors[p])
        iterates[p] = product(thirds(iterates[p]), inverses[p])
    for turn in range(1, NS_ITERS):
        for p in points:
            held = thirds(iterates[p])
            factor = thirds(1.5 * identity - 0.5 * product(inverses[p], held))
            if turn < NS_ITERS - 1:
                iterates[p] = product(held, factor)
            inverses[p] = product(factor, inverses[p])
            if turn < NS_ITERS - 1:
                inverses[p] = thirds(inverses[p])
    for p in points:
        parts = thirds(inverses[p])
        centre = row_product(row_product(right_side[p], parts), parts)[0:1, :] / norms[p]
        weights = inverses[p] * jnp.sqrt((MEMBERS - 1.0) / norms[p]) + centre
        mean = jnp.sum(weights, axis=1, keepdims=True) * (1.0 / MEMBERS)
        mixing[p + 1] = (weights - mean + 1.0 / MEMBERS).astype(jnp.bfloat16)


def analyse_half(half, patch, mixing, result, wide_in, wide_out):
    members = OWN * GROUP
    at = pl.multiple_of(half * HALF, HALF)
    wide_in[...] = patch[:, :, pl.ds(at, HALF)].astype(jnp.float32).reshape(members * LEVELS, HALF)
    first = (half + 1) // 2
    low, high = mixing[first], mixing[first + 1]
    lane = lax.broadcasted_iota(jnp.int32, (1, HALF), 1)
    frac = (lane + jnp.where(half % 2 == 0, HALF, 0)).astype(jnp.float32) / SPACING
    frac = jnp.concatenate([frac, frac], axis=1)
    for tier in range(0, LEVELS, 2):
        field = jnp.concatenate(
            [wide_in[pl.ds(tier + t, members, stride=LEVELS), :] for t in range(2)], axis=1
        ).astype(jnp.bfloat16)
        before = jnp.dot(low, field, preferred_element_type=jnp.float32)
        beyond = jnp.dot(high, field, preferred_element_type=jnp.float32)
        mixed = (1.0 - frac) * before + frac * beyond
        for t in range(2):
            wide_out[pl.ds(tier + t, members, stride=LEVELS), :] = mixed[:, t * HALF : (t + 1) * HALF]
    result[:, :, pl.ds(at, HALF)] = wide_out[...].reshape(members, LEVELS, HALF).astype(jnp.bfloat16)


def encode(facts, active, codes, records):
    site = facts[0:RUNS, :].astype(jnp.int32)
    row = lax.broadcasted_iota(jnp.int32, (RUNS, LANES), 0)
    live = row * LANES + lax.broadcasted_iota(jnp.int32, (RUNS, LANES), 1) < active
    tier = jnp.zeros((RUNS, LANES), jnp.int32)
    for bound in range(1, 2 * LEVELS):
        tier += (site >= bound * CELLS).astype(jnp.int32)
    code = jnp.where(live, tier * 2**PACK + (site - tier * CELLS), -1)
    codes[...] = code
    inverse = jnp.where(live, facts[2 * RUNS : 3 * RUNS, :], 0.0)
    records[...] = jnp.concatenate([facts[RUNS : 2 * RUNS, :], inverse], axis=0)


def cycle_kernel(
    facts,
    active_ref,
    cutoff_ref,
    prior,
    out,
    own,
    patch,
    result,
    codes,
    my_codes,
    records,
    picked,
    arrived,
    lines,
    part_own,
    part_peer,
    window,
    departure,
    columns,
    gram,
    right_side,
    mixing,
    wide_in,
    wide_out,
    send,
    recv,
    part_send,
    part_recv,
    near,
):
    me, level = lax.axis_index("region"), lax.axis_index("level")
    left, right = lax.rem(me + GROUP - 1, GROUP), lax.rem(me + 1, GROUP)
    my_cells = pl.multiple_of(me * CELLS, CELLS)
    order = balanced_order()

    def remote(kind, source, target, peer, tier=level):
        return pltpu.make_async_remote_copy(
            src_ref=source,
            dst_ref=target,
            send_sem=send.at[kind],
            recv_sem=recv.at[kind],
            device_id=(peer, tier),
            device_id_type=MESH,
        )

    def await_bytes(ref, sem):
        pltpu.make_async_copy(ref, ref, sem).wait()

    load_own = pltpu.make_async_copy(prior, own, near.at[0])
    load_own.start()
    load_mine = pltpu.make_async_copy(
        prior.at[:, :, pl.ds(my_cells, CELLS)], patch.at[pl.ds(OWN * me, OWN)], near.at[1]
    )
    load_mine.start()

    barrier = pltpu.get_barrier_semaphore()
    pl.semaphore_signal(barrier, inc=1, device_id=(me, 1 - level), device_id_type=MESH)

    @pl.loop(1, GROUP)
    def _(step):
        pl.semaphore_signal(barrier, inc=1, device_id=(lax.rem(me + step, GROUP), level), device_id_type=MESH)

    encode(facts, active_ref[0], my_codes, records.at[1])
    codes[me, 0:RUNS] = my_codes[...]
    pl.semaphore_wait(barrier, GROUP)

    for offset in order:
        remote(SITES, my_codes, codes.at[me, 0:RUNS], peer_at(me, offset)).start()

    to_right = [remote(RECORD, records.at[1], records.at[0], right)]
    to_left = [remote(RECORD + 1, records.at[1], records.at[2], left)]
    to_right[0].start()
    to_left[0].start()

    width_in = CELLS // PIECES_IN
    messages = [(piece, offset) for piece in range(PIECES_IN) for offset in order]

    def issue(first, last):
        for piece, offset in messages[first:last]:
            peer = peer_at(me, offset)
            at = pl.multiple_of(peer * CELLS + piece * width_in, width_in)
            remote(
                PRIOR + piece,
                prior.at[:, :, pl.ds(at, width_in)],
                patch.at[pl.ds(OWN * me, OWN), :, pl.ds(piece * width_in, width_in)],
                peer,
            ).start()

    issued = FIRST
    issue(0, issued)
    load_own.wait()
    await_bytes(codes.at[pl.ds(0, GROUP - 1), 0:RUNS], recv.at[SITES])
    for quarter in range(4):

        @pl.loop(quarter * GROUP // 4, (quarter + 1) * GROUP // 4)
        def _(region):
            gather_region(region, level, own, codes, picked)

        if quarter < 3:
            issue(issued, issued + LATER)
            issued += LATER

    for offset in order:
        peer = peer_at(me, offset)
        remote(PICKED, picked.at[peer], arrived.at[me], peer).start()

    issue(issued, issued + BETWEEN)
    issued += BETWEEN
    arrived[me] = picked[me]
    await_bytes(arrived.at[pl.ds(0, GROUP - 1)], recv.at[PICKED])
    lines[...] = arrived[...].astype(jnp.float32).reshape(MEMBERS * RUNS, LANES)
    part_own[...] = jnp.concatenate(
        [lines[pl.ds(run, MEMBERS, stride=RUNS), :] for run in range(RUNS)], axis=1
    ).astype(jnp.bfloat16)
    tall = MEMBERS // BLOCKS
    across = []
    for block in range(BLOCKS):
        rows = slice(block * tall, (block + 1) * tall)
        across.append(
            pltpu.make_async_remote_copy(
                src_ref=part_own.at[rows],
                dst_ref=part_peer.at[rows],
                send_sem=part_send.at[block],
                recv_sem=part_recv.at[block],
                device_id=(me, 1 - level),
                device_id_type=MESH,
            )
        )
        across[block].start()
        issue(issued, issued + AMONG_PARTS)
        issued += AMONG_PARTS
    for block in range(BLOCKS):
        rows = slice(block * tall, (block + 1) * tall)
        across[block].wait_recv()
        window[1, rows] = (
            part_own[rows, :].astype(jnp.float32) + part_peer[rows, :].astype(jnp.float32)
        ).astype(jnp.bfloat16)
        remote(HALO, window.at[1, rows], window.at[0, rows], right).start()
        remote(HALO + 1, window.at[1, rows], window.at[2, rows], left).start()
        issue(issued, issued + AMONG_HALOS)
        issued += AMONG_HALOS
    to_right.append(remote(HALO, window.at[1], window.at[0], right))
    to_left.append(remote(HALO + 1, window.at[1], window.at[2], left))
    for copy in to_right + to_left:
        copy.wait_recv()
    issue(issued, len(messages))

    radius = cutoff_ref[0].astype(jnp.float32)
    window_products(window, codes, records, radius, me, departure, columns, gram, right_side)
    ensemble_weights((0, COARSE - 1), gram, right_side, mixing)
    to_right.append(remote(EDGE, mixing.at[COARSE], mixing.at[0], right))
    to_left.append(remote(EDGE + 1, mixing.at[1], mixing.at[COARSE + 1], left))
    to_right[2].start()
    to_left[2].start()
    ensemble_weights((1, 2), gram, right_side, mixing)
    ensemble_weights((3, 4), gram, right_side, mixing)
    to_right[2].wait_recv()
    to_left[2].wait_recv()
    load_mine.wait()
    others = patch.at[pl.ds(0, OWN * (GROUP - 1))]

    per_piece = HALVES // PIECES_OUT
    width = CELLS // PIECES_OUT

    arrivals = [others.at[:, :, pl.ds(piece * width_in, width_in)] for piece in range(PIECES_IN)]
    for group in range(PIECES_IN):
        await_bytes(arrivals[group], recv.at[PRIOR + group])

        @pl.loop(group * PIECES_OUT // PIECES_IN, (group + 1) * PIECES_OUT // PIECES_IN)
        def _(piece):
            @pl.loop(0, per_piece)
            def _(step):
                analyse_half(piece * per_piece + step, patch, mixing, result, wide_in, wide_out)

            at = pl.multiple_of(piece * width, width)
            for offset in order:
                peer = peer_at(me, offset)
                remote(
                    ANALYSIS,
                    result.at[pl.ds(OWN * peer, OWN), :, pl.ds(at, width)],
                    out.at[:, :, pl.ds(pl.multiple_of(my_cells + at, width), width)],
                    peer,
                ).start()

    store_mine = pltpu.make_async_copy(
        result.at[pl.ds(OWN * me, OWN)], out.at[:, :, pl.ds(my_cells, CELLS)], near.at[2]
    )
    store_mine.start()
    await_bytes(codes.at[pl.ds(0, GROUP - 1), 0:RUNS], send.at[SITES])
    await_bytes(arrived.at[pl.ds(0, GROUP - 1)], send.at[PICKED])
    for copy in across:
        copy.wait_send()
    for copy in to_right + to_left:
        copy.wait_send()
    for piece in range(PIECES_IN):
        await_bytes(arrivals[piece], send.at[PRIOR + piece])
    store_mine.wait()
    await_bytes(others, recv.at[ANALYSIS])
    await_bytes(others, send.at[ANALYSIS])


def local(
    prior_samples, measured_site, measured_datum, inverse_variance, active_slots, cutoff_distance
):
    vmem = pl.BlockSpec(memory_space=pltpu.VMEM)
    smem = pl.BlockSpec(memory_space=pltpu.SMEM)
    hbm = pl.BlockSpec(memory_space=pl.ANY)
    block = (MEMBERS, LEVELS, CELLS)
    return pl.pallas_call(
        cycle_kernel,
        out_shape=jax.ShapeDtypeStruct(prior_samples.shape, jnp.bfloat16),
        in_specs=[vmem, smem, smem, hbm],
        out_specs=hbm,
        scratch_shapes=[
            pltpu.VMEM(prior_samples.shape, jnp.bfloat16),
            pltpu.VMEM(block, jnp.bfloat16),
            pltpu.VMEM(block, jnp.bfloat16),
            pltpu.VMEM((GROUP, 2 * RUNS, LANES), jnp.int32),
            pltpu.VMEM((RUNS, LANES), jnp.int32),
            pltpu.VMEM((3, 2 * RUNS, LANES), jnp.float32),
            pltpu.VMEM((GROUP, OWN * RUNS, LANES), jnp.bfloat16),
            pltpu.VMEM((GROUP, OWN * RUNS, LANES), jnp.bfloat16),
            pltpu.VMEM((MEMBERS * RUNS, LANES), jnp.float32),
            pltpu.VMEM((MEMBERS, SLOTS), jnp.bfloat16),
            pltpu.VMEM((MEMBERS, SLOTS), jnp.bfloat16),
            pltpu.VMEM((3, MEMBERS, SLOTS), jnp.bfloat16),
            pltpu.VMEM((MEMBERS, 3 * SLOTS), jnp.float32),
            pltpu.VMEM((8, 3 * SLOTS), jnp.float32),
            pltpu.VMEM((COARSE, MEMBERS, MEMBERS), jnp.float32),
            pltpu.VMEM((COARSE, 16, MEMBERS), jnp.float32),
            pltpu.VMEM((COARSE + 2, MEMBERS, MEMBERS), jnp.bfloat16),
            pltpu.VMEM((MEMBERS * LEVELS, HALF), jnp.float32),
            pltpu.VMEM((MEMBERS * LEVELS, HALF), jnp.float32),
            pltpu.SemaphoreType.DMA((KINDS,)),
            pltpu.SemaphoreType.DMA((KINDS,)),
            pltpu.SemaphoreType.DMA((BLOCKS,)),
            pltpu.SemaphoreType.DMA((BLOCKS,)),
            pltpu.SemaphoreType.DMA((3,)),
        ],
        compiler_params=pltpu.CompilerParams(
            collective_id=0, has_side_effects=True, vmem_limit_bytes=44 * 2**20
        ),
    )(
        jnp.concatenate([measured_site.astype(jnp.float32), measured_datum, inverse_variance]).reshape(
            3 * RUNS, LANES
        ),
        active_slots,
        cutoff_distance,
        prior_samples,
    )


def solution(mesh):
    return jax.shard_map(
        local,
        mesh=mesh,
        in_specs=(
            P("region", "level", None),
            P("region"),
            P("region"),
            P("region"),
            P("region"),
            P("region"),
        ),
        out_specs=P("region", "level", None),
        check_vma=False,
    )
```
